128 devices in a mesh: ctx: 8 (over x_hi, z), head: 4 (over y), ret: 4 (over x_lo, core).
Axes of the slice: x: 4 (x_hi: 2, x_lo: 2; x = x_hi * 2 + x_lo), y: 4, z: 4, core: 2. Of those that a mesh axis runs over, the one named last changes fastest.
Arguments:
- self_query: bfloat16 [4, 1024, 4096], P('ret', 'ctx', 'head'), may hold values from -2.5 to 2.5
- self_key: bfloat16 [4, 1024, 4096], P('ret', 'ctx', 'head'), may hold values from -2.5 to 2.5
- self_value: bfloat16 [4, 1024, 4096], P('ret', 'ctx', 'head'), may hold values from -6 to 6
- self_grad: bfloat16 [4, 1024, 4096], P('ret', 'ctx', 'head'), may hold values from -192 to 192
- self_docs: int32 [4, 1024], P('ret', 'ctx'), may hold values from 0 to 3, never falling along the last dimension, each value on 1 to 512 neighbouring positions
- cross_query: bfloat16 [4, 1024, 4096], P('ret', 'ctx', 'head'), may hold values from -2.5 to 2.5
- cross_grad: bfloat16 [4, 1024, 4096], P('ret', 'ctx', 'head'), may hold values from -96 to 96
- neighbours: int32 [4, 16, 2], P('ret', 'ctx'), may hold values from 0 to 127, as said below
- encodings: bfloat16 [1024, 128, 512], P(('ctx', 'head', 'ret')), may hold values from -6 to 6
- key_weight: bfloat16 [512, 4096], P(None, 'head'), may hold values from -0.25 to 0.25
- value_weight: bfloat16 [512, 4096], P(None, 'head'), may hold values from -0.25 to 0.25
Outputs:
- query_grad: bfloat16 [4, 1024, 4096], P('ret', 'ctx', 'head')
- key_grad: bfloat16 [4, 1024, 4096], P('ret', 'ctx', 'head')
- value_grad: bfloat16 [4, 1024, 4096], P('ret', 'ctx', 'head')
- cross_query_grad: bfloat16 [4, 1024, 4096], P('ret', 'ctx', 'head')
- encoding_grad: bfloat16 [1024, 128, 512], P(('ctx', 'head', 'ret'))
The draws below stay inside these ranges and needn't reach their ends.
Inputs may be any that keep to these rules, and one draw needn't show every extreme that they name: `self_docs`: document numbers never fall along a sequence; each document has 1 to 512 tokens. `neighbours`: an entry v of a span in context block g names pool row g * 16 * 8 + v, held by owner v // 8 of that block (owners counted over head, then ret). Among the 4 entries of one sequence's context block, at most 2 name the same owner. The 2 entries of a span differ.
All inputs are finite; a program needn't handle non-finite values.
Results may differ from the reference program's by a relative error of at most 0.0073.
Values may be sent and summed in bfloat16 or wider, within the bound.
A program may use at most 128 MiB of HBM per device.

```python
import math
import jax
import jax.numpy as jnp
import numpy as np
from jax import lax

SPAN = 64
NBR = 2
NR = 128
E = 512
HEADS = 32
DH = 128
POOL_DEV = 8
CAP = 2
HD = 4096
LENGTH = 1024
SEQS = 4
SPANS_DEV = 2
SPANS = 16
OWNERS = 16
POOL = 1024
N_CTX = 8
N_HEAD = 4
N_RET = 4


def draw_neighbours(key, part):
    key = jax.random.fold_in(key, 7)
    owners_count = N_HEAD * N_RET
    blocks = N_CTX
    requests = SPANS_DEV * NBR
    spare = (owners_count - 1) * CAP
    key_hot, key_pick, key_order, key_first, key_offset = jax.random.split(key, 5)
    hottest = jax.random.randint(key_hot, (blocks,), 0, owners_count)
    base = jnp.arange(spare, dtype=jnp.int32) // CAP
    others = base[None, :] + (base[None, :] >= hottest[:, None]).astype(jnp.int32)
    others = jnp.broadcast_to(others[None], (SEQS, blocks, spare))
    picking = jax.random.randint(key_pick, (SEQS, blocks, spare), 0, 1 << 20) * spare + jnp.arange(spare, dtype=jnp.int32)
    chosen = jnp.take_along_axis(others, jnp.argsort(picking, axis=-1)[..., :requests - CAP], axis=-1)
    owners = jnp.concatenate([jnp.broadcast_to(hottest[None, :, None], (SEQS, blocks, CAP)), chosen], axis=-1)
    ordering = jax.random.randint(key_order, (SEQS, blocks, requests), 0, 1 << 20) * requests + jnp.arange(requests, dtype=jnp.int32)
    owners = jnp.take_along_axis(owners, jnp.argsort(ordering, axis=-1), axis=-1).reshape(SEQS, SPANS, NBR)
    first_row = jax.random.randint(key_first, (SEQS, SPANS), 0, POOL_DEV)
    offsets = jax.random.randint(key_offset, (SEQS, SPANS), 1, POOL_DEV)
    local_rows = jnp.stack([first_row, (first_row + offsets) % POOL_DEV], axis=-1)
    return (owners * POOL_DEV + local_rows).astype(jnp.int32)


def levels(own_key, extent, pieces, smallest, largest):
    factor_of = 1.0
    for axis_at, parts in pieces:
        heights = jax.random.uniform(jax.random.fold_in(jax.random.fold_in(own_key, 6), axis_at), (parts,), jnp.float32, smallest / len(pieces), largest / len(pieces))
        factor_of = factor_of * jnp.repeat(jnp.exp(heights), extent[axis_at] // parts).reshape((-1,) + (1,) * (len(extent) - 1 - axis_at))
    return factor_of


def length_profile(count, total, reach, lean):
    weights = [(1 << 20) // math.isqrt(rank ** lean) + 1 for rank in range(2, count + 1)]
    spare, counts = total - reach - (count - 1), [1] * (count - 1)
    while spare > 0:
        candidates = [i for i in range(count - 1) if counts[i] < reach]
        whole, left = sum([weights[i] for i in candidates]), spare
        for i in candidates:
            addition = min(reach - counts[i], max(1, left * weights[i] // whole), spare)
            counts[i] = counts[i] + addition
            spare = spare - addition
    return np.array([reach] + counts)


def ragged_sizes(own_key, count, total, most, skew):
    if count == 2:
        one = jax.random.randint(own_key, (), max(1, total - most), min(most, total - 1) + 1)
        return jnp.stack([one, total - one])
    sizes = jnp.asarray(length_profile(count, total, most, skew), jnp.int32)
    pairs = (count - 1) // 2
    donor, receiver = sizes[1:1 + 2 * pairs:2], sizes[2:2 + 2 * pairs:2]
    slack = jnp.minimum(donor - 1, most - receiver)
    passed = jax.random.randint(jax.random.fold_in(own_key, 1), (pairs,), 0, 1 << 20) % (slack + 1)
    sizes = sizes.at[1:1 + 2 * pairs:2].set(donor - passed).at[2:2 + 2 * pairs:2].set(receiver + passed)
    return sizes[jax.random.permutation(jax.random.fold_in(own_key, 2), count)]


def normal_values(key, extent, spread, bound, cuts=(), held_as=jnp.bfloat16):
    loudness = levels(key, extent, cuts, -0.22, 0.18) if cuts else 1.0
    values = jax.random.normal(key, extent, jnp.float32) * spread * loudness
    return jnp.minimum(jnp.maximum(values, -bound), bound).astype(held_as)


def setup_inputs(seed: int = 0) -> dict:
    key_of = jax.random.split(jax.random.key(seed), 12)
    return {
        "self_query": normal_values(key_of[0], (SEQS, LENGTH, HD), 1.0, 2.5, ((0, 4), (1, 8), (2, 4))),
        "self_key": normal_values(key_of[1], (SEQS, LENGTH, HD), 1.0, 2.5, ((0, 4), (1, 8), (2, 4))),
        "self_value": normal_values(key_of[2], (SEQS, LENGTH, HD), 1.0, 6.0, ((0, 4), (1, 8), (2, 4))),
        "self_grad": normal_values(key_of[3], (SEQS, LENGTH, HD), 32.0, 192.0, ((0, 4), (1, 8), (2, 4))),
        "self_docs": jax.vmap(lambda own: jnp.searchsorted(jnp.cumsum(ragged_sizes(own, 4, LENGTH, LENGTH // 2, 0)), jnp.arange(LENGTH), side="right"))(jax.random.split(key_of[4], SEQS)).reshape((SEQS, LENGTH)).astype(jnp.int32),
        "cross_query": normal_values(key_of[5], (SEQS, LENGTH, HD), 1.0, 2.5, ((0, 4), (1, 8), (2, 4))),
        "cross_grad": normal_values(key_of[6], (SEQS, LENGTH, HD), 16.0, 96.0, ((0, 4), (1, 8), (2, 4))),
        "neighbours": draw_neighbours(jax.random.fold_in(key_of[11], 71), 0),
        "encodings": normal_values(key_of[8], (POOL, NR, E), 1.0, 6.0, ((0, 128),)),
        "key_weight": normal_values(key_of[9], (E, HD), E ** -0.5, 0.25, ((1, 4),)),
        "value_weight": normal_values(key_of[10], (E, HD), E ** -0.5, 0.25, ((1, 4),)),
    }


EPSILON = 1e-06

def widened(values):
    return lax.optimization_barrier(values).astype(jnp.float32)

def self_head(queries, keys_rows, values_rows, grads_rows, documents):
    length = queries.shape[0]
    score_scale = 1.0 / math.sqrt(queries.shape[1])
    places = jnp.arange(length, dtype=jnp.int32)
    visible = (places[None, :] <= places[:, None]) & (documents[None, :] == documents[:, None])
    scores = jnp.dot(queries, keys_rows.T, preferred_element_type=jnp.float32) * score_scale
    raw_weights = jnp.where(visible, jnp.exp(scores), 0.0)
    totals = lax.optimization_barrier(jnp.sum(raw_weights, axis=1))
    numerator = jnp.dot(raw_weights.astype(jnp.bfloat16), values_rows, preferred_element_type=jnp.float32)
    deltas = lax.optimization_barrier(jnp.sum(grads_rows.astype(jnp.float32) * numerator, axis=1)) / totals
    normed = raw_weights / totals[:, None]
    dnormed = jnp.dot(grads_rows, values_rows.T, preferred_element_type=jnp.float32)
    dscores = (normed * (dnormed - deltas[:, None])).astype(jnp.bfloat16)
    query_part = jnp.dot(dscores, keys_rows, preferred_element_type=jnp.float32) * score_scale
    key_part = jnp.dot(dscores.T, queries, preferred_element_type=jnp.float32) * score_scale
    value_part = jnp.dot(normed.astype(jnp.bfloat16).T, grads_rows, preferred_element_type=jnp.float32)
    return (query_part.astype(jnp.bfloat16), key_part.astype(jnp.bfloat16), value_part.astype(jnp.bfloat16))

def cross_span(span_queries, span_grads, gathered, key_weight, value_weight):
    score_scale = 1.0 / math.sqrt(DH)
    keys_raw = jnp.dot(gathered, key_weight, preferred_element_type=jnp.float32).reshape(NBR * NR, HEADS, DH)
    factor = lax.rsqrt(lax.optimization_barrier(jnp.mean(keys_raw * keys_raw, axis=2, keepdims=True)) + EPSILON)
    keys_n = keys_raw * factor
    keys_b = widened(keys_n.astype(jnp.bfloat16))
    values_b = widened(jnp.dot(gathered, value_weight, preferred_element_type=jnp.float32).astype(jnp.bfloat16).reshape(NBR * NR, HEADS, DH))
    queries_f = span_queries.reshape(SPAN, HEADS, DH).astype(jnp.float32)
    grads_f = span_grads.reshape(SPAN, HEADS, DH).astype(jnp.float32)
    scores = jnp.einsum('qhd,khd->hqk', queries_f, keys_b) * score_scale
    raw_weights = jnp.exp(scores)
    cprobs = raw_weights / lax.optimization_barrier(jnp.sum(raw_weights, axis=2, keepdims=True))
    cprobs_b = widened(cprobs.astype(jnp.bfloat16))
    couts = jnp.einsum('hqk,khd->qhd', cprobs_b, values_b)
    cdeltas = jnp.einsum('qhd,qhd->hq', grads_f, couts)
    dprobs = jnp.einsum('qhd,khd->hqk', grads_f, values_b)
    cdscores = widened((cprobs * (dprobs - cdeltas[:, :, None])).astype(jnp.bfloat16))
    query_part = jnp.einsum('hqk,khd->qhd', cdscores, keys_b) * score_scale
    grad_keys_n = jnp.einsum('hqk,qhd->khd', cdscores, queries_f) * score_scale
    grad_values = jnp.einsum('hqk,qhd->khd', cprobs_b, grads_f)
    grad_raw = factor * (grad_keys_n - keys_n * lax.optimization_barrier(jnp.mean(keys_n * grad_keys_n, axis=2, keepdims=True)))
    partial_grad = jnp.dot(grad_raw.astype(jnp.bfloat16).reshape(NBR * NR, HD), key_weight.T, preferred_element_type=jnp.float32)
    partial_grad = partial_grad + jnp.dot(grad_values.astype(jnp.bfloat16).reshape(NBR * NR, HD), value_weight.T, preferred_element_type=jnp.float32)
    return (query_part.reshape(SPAN, HD).astype(jnp.bfloat16), partial_grad.reshape(NBR, NR, E))

def to_heads(array):
    return array.reshape(SEQS, LENGTH, HEADS, DH).transpose(0, 2, 1, 3).reshape(SEQS * HEADS, LENGTH, DH)

def from_heads(array):
    return array.reshape(SEQS, HEADS, LENGTH, DH).transpose(0, 2, 1, 3).reshape(SEQS, LENGTH, HD)

def reference(self_query, self_key, self_value, self_grad, self_docs, cross_query, cross_grad, neighbours, encodings, key_weight, value_weight):
    stacked = (to_heads(self_query), to_heads(self_key), to_heads(self_value), to_heads(self_grad), jnp.repeat(self_docs, HEADS, axis=0))
    query_heads, key_heads, value_heads = lax.map(lambda inputs: self_head(*inputs), stacked)
    block_of = jnp.arange(SPANS, dtype=jnp.int32) // SPANS_DEV
    pool_rows = (neighbours + (block_of * (OWNERS * POOL_DEV))[None, :, None]).astype(jnp.int32).reshape(SEQS * SPANS, NBR)
    span_queries = cross_query.reshape(SEQS * SPANS, SPAN, HD)
    span_grads = cross_grad.reshape(SEQS * SPANS, SPAN, HD)

    def one_span(inputs):
        queries_here, grads_here, rows_here = inputs
        gathered = jnp.take(encodings, rows_here, axis=0).reshape(NBR * NR, E)
        return cross_span(queries_here, grads_here, gathered, key_weight, value_weight)
    cross_parts, partials = lax.map(one_span, (span_queries, span_grads, pool_rows))
    encoding_sum = jnp.zeros((POOL, NR, E), jnp.float32).at[pool_rows.reshape(-1)].add(partials.reshape(SEQS * SPANS * NBR, NR, E))
    return (from_heads(query_heads), from_heads(key_heads), from_heads(value_heads), cross_parts.reshape(SEQS, LENGTH, HD), encoding_sum.astype(jnp.bfloat16))
```

```python
import functools
import math

import jax
import jax.numpy as jnp
from jax import lax
from jax.experimental import pallas as pl
from jax.experimental.pallas import tpu as pltpu
from jax.sharding import PartitionSpec as P

SPAN = 64
NBR = 2
NR = 128
E = 512
DH = 128
POOL_DEV = 8
EPSILON = 1e-06
SCALE = 1.0 / math.sqrt(DH)

N_CTX = 8
N_HEAD = 4
N_RET = 4
ENTRIES = 4
BLOCK = 128
TILE = 256
QUARTER = E // N_HEAD
CHUNKS = 2
CHUNK = NR // CHUNKS
FINAL = 2
FINAL_ROWS = NR // FINAL

MESH = pl.DeviceIdType.MESH
F32 = jnp.float32
BF16 = jnp.bfloat16


def dot(a, b):
    return lax.dot_general(a, b, (((1,), (0,)), ((), ())), preferred_element_type=F32)


def dot_nt(a, b):
    return lax.dot_general(a, b, (((1,), (1,)), ((), ())), preferred_element_type=F32)


def kernel(
    sq, sk, sv, sg, docs, cq, cg, nbr, enc, wk, wv,
    oq, ok, ov, ocq, oenc,
    lists_v, lists_s, docs_v, doc_cols, pool, outgoing, incoming, rows, held, key_acc, value_acc, grads,
    wk_v, wv_v, cq_v, cg_v, cross_out, partial, parts_out, parts_in, shares, owned,
    loc, s_list, r_list, s_docs, r_docs, s_pool, r_pool, s_ret, r_ret, s_rows, r_rows, s_self, r_self,
    s_part, r_part, s_share, r_share, s_own, r_own, s_back, r_back,
):
    c, h, r = lax.axis_index("ctx"), lax.axis_index("head"), lax.axis_index("ret")

    def over_ctx(d):
        return lax.rem(c + d, N_CTX)

    def over_head(d):
        return lax.rem(h + d, N_HEAD)

    def over_ret(d):
        return lax.rem(r + d, N_RET)

    def send(src, dst, ssem, rsem, device):
        copy = pltpu.make_async_remote_copy(
            src_ref=src, dst_ref=dst, send_sem=ssem, recv_sem=rsem,
            device_id=device, device_id_type=MESH,
        )
        copy.start()
        return copy

    local_count = [0]

    def keep(src, dst):
        copy = pltpu.make_async_copy(src, dst, loc.at[local_count[0]])
        local_count[0] += 1
        copy.start()
        return copy

    sent = []

    lane = lax.broadcasted_iota(jnp.int32, (8, 128), 1)
    tile = jnp.zeros((8, 128), jnp.int32)
    for e in range(ENTRIES):
        tile = jnp.where(lane == e, nbr[0, e // NBR, e % NBR], tile)
    lists_v[r] = tile

    barrier = pltpu.get_barrier_semaphore()
    peers = [(over_ctx(d), h, r) for d in range(1, N_CTX)]
    peers += [(c, over_head(d), r) for d in range(1, N_HEAD)]
    peers += [(c, h, over_ret(d)) for d in range(1, N_RET)]
    for peer in peers:
        pl.semaphore_signal(barrier, inc=1, device_id=peer, device_id_type=MESH)
    pl.semaphore_wait(barrier, len(peers))

    list_copies = [
        send(lists_v.at[r], lists_v.at[r], s_list.at[d - 1], r_list.at[d - 1], (c, h, over_ret(d)))
        for d in range(1, N_RET)
    ]

    def quarter_of(owner_column, t):
        return enc.at[:, pl.ds(t * CHUNK, CHUNK), pl.ds(pl.multiple_of(owner_column * QUARTER, 128), QUARTER)]

    pool_copies = []
    pool_own = []
    for t in range(CHUNKS):
        pool_copies.append([
            send(
                quarter_of(over_head(d), t),
                pool[t].at[pl.ds(h * POOL_DEV, POOL_DEV)],
                s_pool.at[t * 3 + d - 1], r_pool.at[t * 3 + d - 1], (c, over_head(d), r),
            )
            for d in (2, 1, 3)
        ])
        pool_own.append(
            keep(quarter_of(h, t), pool[t].at[pl.ds(h * POOL_DEV, POOL_DEV)])
        )
    doc_copies = [
        send(docs, docs_v.at[c], s_docs.at[d - 1], r_docs.at[d - 1], (over_ctx(d), h, r))
        for d in range(1, N_CTX)
    ]
    doc_own = keep(docs, docs_v.at[c])
    self_in = (sq, sk, sv, sg)

    def head_of(array, number):
        return array.at[0, :, pl.ds(pl.multiple_of(number * DH, 128), DH)]

    self_copies = []
    for d in (6, 2, 5, 3, 7, 1, 4):
        for a in range(4):
            at = (d - 1) * 4 + a
            self_copies.append(send(
                head_of(self_in[a], over_ctx(d)),
                held.at[a, pl.ds(pl.multiple_of(c * BLOCK, 128), BLOCK)],
                s_self.at[at], r_self.at[at], (over_ctx(d), h, r),
            ))
    self_own = [
        keep(head_of(self_in[a], c), held.at[a, pl.ds(pl.multiple_of(c * BLOCK, 128), BLOCK)])
        for a in range(4)
    ]
    cross_own = [keep(wk, wk_v), keep(wv, wv_v), keep(cq.at[0], cq_v), keep(cg.at[0], cg_v)]

    for copy in list_copies:
        copy.wait_recv()
    sent.extend(list_copies)
    to_scalars = keep(lists_v, lists_s)
    to_scalars.wait()

    ret_copies = []
    for t in range(CHUNKS):
        here = pl.ds(t * CHUNK, CHUNK)
        pool_own[t].wait()
        for copy in pool_copies[t]:
            copy.wait_recv()
        sent.extend(pool_copies[t])
        for q in range(N_RET):
            for e in range(ENTRIES):
                value = lists_s[q, 0, e]
                place = lax.div(value, N_RET * POOL_DEV) * POOL_DEV + lax.rem(value, POOL_DEV)
                outgoing[q * ENTRIES + e, here] = pool[t][place]
        own = [
            keep(
                outgoing.at[pl.ds(r * ENTRIES, ENTRIES), here],
                incoming[t].at[pl.ds(r * ENTRIES, ENTRIES)],
            )
        ]
        ret_copies.append((own, [
            send(
                outgoing.at[pl.ds(over_ret(d) * ENTRIES, ENTRIES), here],
                incoming[t].at[pl.ds(r * ENTRIES, ENTRIES)],
                s_ret.at[t * 3 + d - 1], r_ret.at[t * 3 + d - 1], (c, h, over_ret(d)),
            )
            for d in (2, 1, 3)
        ]))

    row_copies = []
    my_columns = pl.ds(pl.multiple_of(h * QUARTER, 128), QUARTER)
    for t in range(CHUNKS):
        here = pl.ds(t * CHUNK, CHUNK)
        own, copies = ret_copies[t]
        for copy in own:
            copy.wait()
        for copy in copies:
            copy.wait_recv()
        sent.extend(copies)
        for e in range(ENTRIES):
            value = lists_s[r, 0, e]
            column = lax.rem(lax.div(value, POOL_DEV), N_RET)
            rows[e, here, my_columns] = incoming[t][column * ENTRIES + e]
        row_copies.append([
            send(
                rows.at[:, here, my_columns], rows.at[:, here, my_columns],
                s_rows.at[t * 3 + d - 1], r_rows.at[t * 3 + d - 1], (c, over_head(d), r),
            )
            for d in (2, 1, 3)
        ])

    for copy in cross_own:
        copy.wait()
    for copies in row_copies:
        for copy in copies:
            copy.wait_recv()
        sent.extend(copies)

    lanes = lax.broadcasted_iota(jnp.int32, (SPAN, TILE), 1)

    def paired(block):
        low = jnp.where(lanes < DH, block, jnp.zeros_like(block))
        high = jnp.where(lanes >= DH, block, jnp.zeros_like(block))
        return jnp.concatenate([low, high], axis=0)

    def cross_span(s):
        tokens = rows[s * NBR:(s + 1) * NBR].reshape(NBR * NR, E)
        here = slice(s * SPAN, (s + 1) * SPAN)
        for p in range(4):
            cols = slice(p * TILE, (p + 1) * TILE)
            keys_raw = dot(tokens, wk_v[:, cols])
            values_b = dot(tokens, wv_v[:, cols]).astype(BF16)
            factors, normed = [], []
            for a in range(2):
                one = keys_raw[:, a * DH:(a + 1) * DH]
                factor = lax.rsqrt(jnp.sum(one * one, axis=1, keepdims=True) * (1.0 / DH) + EPSILON)
                factors.append(factor)
                normed.append(one * factor)
            keys_b = jnp.concatenate([n.astype(BF16) for n in normed], axis=1)
            query = paired(cq_v[here, cols])
            grad = paired(cg_v[here, cols])
            raw = jnp.exp(dot_nt(keys_b, query) * SCALE)
            probs = raw * (1.0 / jnp.sum(raw, axis=0, keepdims=True))
            probs_b = probs.astype(BF16)
            dprobs = dot_nt(values_b, grad)
            cdeltas = jnp.sum(probs_b.astype(F32) * dprobs, axis=0, keepdims=True)
            dscores = probs * (dprobs - cdeltas)
            dscores_b = dscores.astype(BF16)
            query_part = dot(dscores.T.astype(BF16), keys_b) * SCALE
            cross_out[here, p * TILE:p * TILE + DH] = query_part[:SPAN, :DH].astype(BF16)
            cross_out[here, p * TILE + DH:(p + 1) * TILE] = query_part[SPAN:, DH:].astype(BF16)
            grad_keys = dot(dscores_b, query) * SCALE
            grad_values = dot(probs_b, grad).astype(BF16)
            raws = []
            for a in range(2):
                one = grad_keys[:, a * DH:(a + 1) * DH]
                mean = jnp.sum(normed[a] * one, axis=1, keepdims=True) * (1.0 / DH)
                raws.append((factors[a] * (one - normed[a] * mean)).astype(BF16))
            grad_raw = jnp.concatenate(raws, axis=1)
            term = dot_nt(grad_raw, wk_v[:, cols]) + dot_nt(grad_values, wv_v[:, cols])
            if p == 0:
                partial[...] = term
            else:
                partial[...] += term
        for q in range(N_HEAD):
            parts_out[q, s * NBR * NR:(s + 1) * NBR * NR] = partial[:, q * QUARTER:(q + 1) * QUARTER].astype(BF16)
        span_rows = pl.ds(s * NBR * NR, NBR * NR)
        return [
            send(
                parts_out.at[over_head(d), span_rows], parts_in.at[h, span_rows],
                s_part.at[s * 3 + d - 1], r_part.at[s * 3 + d - 1], (c, over_head(d), r),
            )
            for d in (2, 1, 3)
        ]

    part_copies = [cross_span(s) for s in range(2)]
    cross_done = keep(cross_out, ocq.at[0])

    def share_span(s):
        span_rows = slice(s * NBR * NR, (s + 1) * NBR * NR)
        for copy in part_copies[s]:
            copy.wait_recv()
        sent.extend(part_copies[s])
        total = parts_out[h, span_rows].astype(F32)
        for d in range(1, N_HEAD):
            total = total + parts_in[over_head(d), span_rows].astype(F32)
        mine = pl.ds(r * ENTRIES + s * NBR, NBR)
        shares[mine] = total.astype(BF16).reshape(NBR, NR, QUARTER)
        return [
            send(
                shares.at[mine], shares.at[mine],
                s_share.at[s * 3 + d - 1], r_share.at[s * 3 + d - 1], (c, h, over_ret(d)),
            )
            for d in (2, 1, 3)
        ]

    def prepare_self():
        doc_own.wait()
        for copy in doc_copies + self_copies:
            copy.wait_recv()
        for copy in self_own:
            copy.wait()
        sent.extend(doc_copies + self_copies)
        for b in range(N_CTX):
            one = jnp.broadcast_to(docs_v[b].astype(F32), (BLOCK, BLOCK))
            doc_cols[b * BLOCK:(b + 1) * BLOCK] = one.T

    key_at = lax.broadcasted_iota(jnp.int32, (TILE, TILE), 0)
    query_at = lax.broadcasted_iota(jnp.int32, (TILE, TILE), 1)

    def self_rows(i):
        mine = slice(i * TILE, (i + 1) * TILE)
        query, grad = held[0, mine], held[3, mine]
        query_docs = jnp.concatenate([docs_v[2 * i], docs_v[2 * i + 1]], axis=1).astype(F32)
        first = max(0, i - 2)
        totals = jnp.zeros((1, TILE), F32)
        deltas = jnp.zeros((1, TILE), F32)
        raws, dnormeds = [], []
        for j in range(first, i + 1):
            there = slice(j * TILE, (j + 1) * TILE)
            key_docs = doc_cols[there]
            visible = jnp.concatenate([key_docs, key_docs], axis=1) == query_docs
            if j == i:
                visible = visible & (key_at <= query_at)
            raw = jnp.where(visible, jnp.exp(dot_nt(held[1, there], query) * SCALE), 0.0)
            dnormed = dot_nt(held[2, there], grad)
            totals = totals + jnp.sum(raw, axis=0, keepdims=True)
            deltas = deltas + jnp.sum(raw.astype(BF16).astype(F32) * dnormed, axis=0, keepdims=True)
            raws.append(raw)
            dnormeds.append(dnormed)
        inverse = 1.0 / totals
        deltas = deltas * inverse
        query_sum = jnp.zeros((DH, TILE), F32)
        for j in range(first, i + 1):
            there = slice(j * TILE, (j + 1) * TILE)
            normed = raws[j - first] * inverse
            dscores = (normed * (dnormeds[j - first] - deltas)).astype(BF16)
            query_sum = query_sum + dot(held[1, there].astype(F32).T.astype(BF16), dscores)
            key_term = dot(dscores, query)
            value_term = dot(normed.astype(BF16), grad)
            if j == i:
                key_acc[there] = key_term
                value_acc[there] = value_term
            else:
                key_acc[there] += key_term
                value_acc[there] += value_term
        grads[0, mine] = (query_sum * SCALE).T.astype(BF16)

    def self_back():
        outs = (oq, ok, ov)
        copies = []
        for d in (6, 2, 5, 3, 7, 1, 4):
            for a in range(3):
                at = (d - 1) * 3 + a
                copies.append(send(
                    grads.at[a, pl.ds(pl.multiple_of(over_ctx(d) * BLOCK, 128), BLOCK)],
                    head_of(outs[a], c),
                    s_back.at[at], r_back.at[at], (over_ctx(d), h, r),
                ))
        own = [
            keep(grads.at[a, pl.ds(pl.multiple_of(c * BLOCK, 128), BLOCK)], head_of(outs[a], c))
            for a in range(3)
        ]
        return copies, own

    prepare_self()
    self_rows(0)
    share_copies = [share_span(0)]
    self_rows(1)
    share_copies.append(share_span(1))
    self_rows(2)
    self_rows(3)
    grads[1] = (key_acc[...] * SCALE).astype(BF16)
    grads[2] = value_acc[...].astype(BF16)
    back_copies, back_own = self_back()

    for copies in share_copies:
        for copy in copies:
            copy.wait_recv()
        sent.extend(copies)

    GROUP = 16
    lane_e = lax.broadcasted_iota(jnp.int32, (1, N_RET * ENTRIES * GROUP), 1)
    named = jnp.zeros((1, N_RET * ENTRIES * GROUP), jnp.int32)
    for q in range(N_RET):
        for e in range(ENTRIES):
            k = q * ENTRIES + e
            named = jnp.where(lane_e // GROUP == k, lists_s[q, 0, e], named)
    wide = (N_HEAD * POOL_DEV * GROUP, N_RET * ENTRIES * GROUP)
    target = lax.broadcasted_iota(jnp.int32, wide, 0)
    slot = target // GROUP
    wanted = ((slot // POOL_DEV) * N_RET + r) * POOL_DEV + slot % POOL_DEV
    same_token = target % GROUP == lax.broadcasted_iota(jnp.int32, wide, 1) % GROUP
    selector = jnp.where((wanted == named) & same_token, 1.0, 0.0).astype(BF16)

    own_copies = []
    own_kept = []
    for f in range(FINAL):
        for t in range(FINAL_ROWS // GROUP):
            at = slice(f * FINAL_ROWS + t * GROUP, f * FINAL_ROWS + (t + 1) * GROUP)
            stacked = shares[:, at].reshape(N_RET * ENTRIES * GROUP, QUARTER)
            summed = dot(selector, stacked)
            owned[:, at] = summed.astype(BF16).reshape(N_HEAD * POOL_DEV, GROUP, QUARTER)
        here = pl.ds(f * FINAL_ROWS, FINAL_ROWS)
        for d in (2, 1, 3):
            own_copies.append(send(
                owned.at[pl.ds(over_head(d) * POOL_DEV, POOL_DEV), here], oenc.at[:, here, my_columns],
                s_own.at[f * 3 + d - 1], r_own.at[f * 3 + d - 1], (c, over_head(d), r),
            ))
        own_kept.append(keep(owned.at[pl.ds(h * POOL_DEV, POOL_DEV), here], oenc.at[:, here, my_columns]))

    cross_done.wait()
    for copy in back_own + own_kept:
        copy.wait()
    for copy in back_copies + own_copies:
        copy.wait_recv()
    sent.extend(back_copies + own_copies)
    for copy in sent:
        copy.wait_send()


def on_device(
    self_query, self_key, self_value, self_grad, self_docs, cross_query, cross_grad,
    neighbours, encodings, key_weight, value_weight,
):
    block = jax.ShapeDtypeStruct(self_query.shape, BF16)
    any_space = pl.BlockSpec(memory_space=pltpu.HBM)
    in_specs = [any_space] * 11
    in_specs[7] = pl.BlockSpec(memory_space=pltpu.SMEM)
    dma = pltpu.SemaphoreType.DMA
    scratch = [
        pltpu.VMEM((N_RET, 8, 128), jnp.int32),
        pltpu.SMEM((N_RET, 8, 128), jnp.int32),
        pltpu.VMEM((N_CTX, 1, BLOCK), jnp.int32),
        pltpu.VMEM((N_CTX * BLOCK, 128), F32),
        (pltpu.VMEM((N_HEAD * POOL_DEV, CHUNK, QUARTER), BF16),) * CHUNKS,
        pltpu.VMEM((N_RET * ENTRIES, NR, QUARTER), BF16),
        (pltpu.VMEM((N_RET * ENTRIES, CHUNK, QUARTER), BF16),) * CHUNKS,
        pltpu.VMEM((ENTRIES, NR, E), BF16),
        pltpu.VMEM((4, N_CTX * BLOCK, DH), BF16),
        pltpu.VMEM((N_CTX * BLOCK, DH), F32),
        pltpu.VMEM((N_CTX * BLOCK, DH), F32),
        pltpu.VMEM((3, N_CTX * BLOCK, DH), BF16),
        pltpu.VMEM(key_weight.shape, BF16),
        pltpu.VMEM(value_weight.shape, BF16),
        pltpu.VMEM(cross_query.shape[1:], BF16),
        pltpu.VMEM(cross_grad.shape[1:], BF16),
        pltpu.VMEM(cross_grad.shape[1:], BF16),
        pltpu.VMEM((NBR * NR, E), F32),
        pltpu.VMEM((N_HEAD, ENTRIES * NR, QUARTER), BF16),
        pltpu.VMEM((N_HEAD, ENTRIES * NR, QUARTER), BF16),
        pltpu.VMEM((N_RET * ENTRIES, NR, QUARTER), BF16),
        pltpu.VMEM((N_HEAD * POOL_DEV, NR, QUARTER), BF16),
        dma((24,)),
        dma((3,)), dma((3,)),
        dma((7,)), dma((7,)),
        dma((3 * CHUNKS,)), dma((3 * CHUNKS,)),
        dma((3 * CHUNKS,)), dma((3 * CHUNKS,)),
        dma((3 * CHUNKS,)), dma((3 * CHUNKS,)),
        dma((28,)), dma((28,)),
        dma((6,)), dma((6,)),
        dma((6,)), dma((6,)),
        dma((3 * FINAL,)), dma((3 * FINAL,)),
        dma((21,)), dma((21,)),
    ]
    return pl.pallas_call(
        kernel,
        out_shape=(block, block, block, block, jax.ShapeDtypeStruct(encodings.shape, BF16)),
        in_specs=in_specs,
        out_specs=(any_space,) * 5,
        scratch_shapes=scratch,
        compiler_params=pltpu.CompilerParams(
            collective_id=0, has_side_effects=True, vmem_limit_bytes=64 * 2**20
        ),
        name="retro_backward",
    )(
        self_query, self_key, self_value, self_grad, self_docs, cross_query, cross_grad,
        neighbours, encodings, key_weight, value_weight,
    )


def solution(mesh):
    tokens = P("ret", "ctx", "head")
    pool = P(("ctx", "head", "ret"), None, None)
    placed = (
        tokens, tokens, tokens, tokens, P("ret", "ctx"), tokens, tokens,
        P("ret", "ctx", None), pool, P(None, "head"), P(None, "head"),
    )
    return jax.shard_map(
        on_device,
        mesh=mesh,
        in_specs=placed,
        out_specs=(tokens, tokens, tokens, tokens, pool),
        check_vma=False,
    )
```

```python
import functools
import math

import jax
import jax.numpy as jnp
from jax import lax
from jax.experimental import pallas as pl
from jax.experimental.pallas import tpu as pltpu
from jax.sharding import PartitionSpec as P

SPAN = 64
NBR = 2
NR = 128
E = 512
DH = 128
POOL_DEV = 8
EPSILON = 1e-06
SCALE = 1.0 / math.sqrt(DH)

N_CTX = 8
N_HEAD = 4
N_RET = 4
ENTRIES = 4
BLOCK = 128
TILE = 256
QUARTER = E // N_HEAD
CHUNKS = 2
CHUNK = NR // CHUNKS

MESH = pl.DeviceIdType.MESH
F32 = jnp.float32
BF16 = jnp.bfloat16


def dot(a, b):
    return lax.dot_general(a, b, (((1,), (0,)), ((), ())), preferred_element_type=F32)


def dot_nt(a, b):
    return lax.dot_general(a, b, (((1,), (1,)), ((), ())), preferred_element_type=F32)


def kernel(
    sq, sk, sv, sg, docs, cq, cg, nbr, enc, wk, wv,
    oq, ok, ov, ocq, oenc,
    lists_v, lists_s, docs_v, doc_cols, pool, outgoing, incoming, rows, held, key_acc, value_acc, grads,
    wk_v, wv_v, cq_v, cg_v, cross_out, keys_n, factors, keys_b, values_b, raw_grads, value_grads, parts_out, parts_in, shares, owned,
    loc, s_list, r_list, s_docs, r_docs, s_pool, r_pool, s_ret, r_ret, s_rows, r_rows, s_self, r_self,
    s_part, r_part, s_share, r_share, s_own, r_own, s_back, r_back,
):
    c, h, r = lax.axis_index("ctx"), lax.axis_index("head"), lax.axis_index("ret")

    def over_ctx(d):
        return lax.rem(c + d, N_CTX)

    def over_head(d):
        return lax.rem(h + d, N_HEAD)

    def over_ret(d):
        return lax.rem(r + d, N_RET)

    def send(src, dst, ssem, rsem, device):
        copy = pltpu.make_async_remote_copy(
            src_ref=src, dst_ref=dst, send_sem=ssem, recv_sem=rsem,
            device_id=device, device_id_type=MESH,
        )
        copy.start()
        every.append(copy)
        return copy

    every = []
    local_count = [0]

    def keep(src, dst):
        copy = pltpu.make_async_copy(src, dst, loc.at[local_count[0]])
        local_count[0] += 1
        copy.start()
        return copy

    lane = lax.broadcasted_iota(jnp.int32, (8, 128), 1)
    tile = jnp.zeros((8, 128), jnp.int32)
    for e in range(ENTRIES):
        tile = jnp.where(lane == e, nbr[0, e // NBR, e % NBR], tile)
    lists_v[r] = tile

    barrier = pltpu.get_barrier_semaphore()
    peers = [(over_ctx(d), h, r) for d in range(1, N_CTX)]
    peers += [(c, over_head(d), r) for d in range(1, N_HEAD)]
    peers += [(c, h, over_ret(d)) for d in range(1, N_RET)]
    for peer in peers:
        pl.semaphore_signal(barrier, inc=1, device_id=peer, device_id_type=MESH)
    pl.semaphore_wait(barrier, len(peers))

    list_copies = [
        send(lists_v.at[r], lists_v.at[r], s_list.at[d - 1], r_list.at[d - 1], (c, h, over_ret(d)))
        for d in range(1, N_RET)
    ]

    def quarter_of(owner_column, t):
        return enc.at[:, pl.ds(t * CHUNK, CHUNK), pl.ds(pl.multiple_of(owner_column * QUARTER, 128), QUARTER)]

    pool_copies = []
    pool_own = []
    for t in range(CHUNKS):
        pool_copies.append([
            send(
                quarter_of(over_head(d), t),
                pool[t].at[pl.ds(h * POOL_DEV, POOL_DEV)],
                s_pool.at[t * 3 + d - 1], r_pool.at[t * 3 + d - 1], (c, over_head(d), r),
            )
            for d in (2, 1, 3)
        ])
        pool_own.append(
            keep(quarter_of(h, t), pool[t].at[pl.ds(h * POOL_DEV, POOL_DEV)])
        )
    doc_copies = [
        send(docs, docs_v.at[c], s_docs.at[d - 1], r_docs.at[d - 1], (over_ctx(d), h, r))
        for d in range(1, N_CTX)
    ]
    doc_own = keep(docs, docs_v.at[c])
    self_in = (sq, sk, sv, sg)

    def head_of(array, number):
        return array.at[0, :, pl.ds(pl.multiple_of(number * DH, 128), DH)]

    self_copies = []
    self_own = []

    def self_start():
        for d in (6, 2, 5, 3, 7, 1, 4):
            for a in range(4):
                at = (d - 1) * 4 + a
                self_copies.append(send(
                    head_of(self_in[a], over_ctx(d)),
                    held.at[a, pl.ds(pl.multiple_of(c * BLOCK, 128), BLOCK)],
                    s_self.at[at], r_self.at[at], (over_ctx(d), h, r),
                ))
        for a in range(4):
            self_own.append(
                keep(head_of(self_in[a], c), held.at[a, pl.ds(pl.multiple_of(c * BLOCK, 128), BLOCK)])
            )

    self_start()
    cross_own = [keep(wk, wk_v), keep(wv, wv_v), keep(cq.at[0], cq_v), keep(cg.at[0], cg_v)]

    for copy in list_copies:
        copy.wait_recv()
    to_scalars = keep(lists_v, lists_s)
    to_scalars.wait()

    ret_copies = []
    for t in range(CHUNKS):
        here = pl.ds(t * CHUNK, CHUNK)
        pool_own[t].wait()
        for copy in pool_copies[t]:
            copy.wait_recv()
        for q in range(N_RET):
            for e in range(ENTRIES):
                value = lists_s[q, 0, e]
                place = lax.div(value, N_RET * POOL_DEV) * POOL_DEV + lax.rem(value, POOL_DEV)
                outgoing[q * ENTRIES + e, here] = pool[t][place]
        own = [
            keep(
                outgoing.at[pl.ds(r * ENTRIES, ENTRIES), here],
                incoming[t].at[pl.ds(r * ENTRIES, ENTRIES)],
            )
        ]
        ret_copies.append((own, [
            send(
                outgoing.at[pl.ds(over_ret(d) * ENTRIES, ENTRIES), here],
                incoming[t].at[pl.ds(r * ENTRIES, ENTRIES)],
                s_ret.at[t * 3 + d - 1], r_ret.at[t * 3 + d - 1], (c, h, over_ret(d)),
            )
            for d in (2, 1, 3)
        ]))

    row_copies = []
    my_columns = pl.ds(pl.multiple_of(h * QUARTER, 128), QUARTER)
    for t in range(CHUNKS):
        here = pl.ds(t * CHUNK, CHUNK)
        own, copies = ret_copies[t]
        for copy in own:
            copy.wait()
        for copy in copies:
            copy.wait_recv()
        for e in range(ENTRIES):
            value = lists_s[r, 0, e]
            column = lax.rem(lax.div(value, POOL_DEV), N_RET)
            rows[e, here, my_columns] = incoming[t][column * ENTRIES + e]
        row_copies.append([
            send(
                rows.at[:, here, my_columns], rows.at[:, here, my_columns],
                s_rows.at[t * 3 + d - 1], r_rows.at[t * 3 + d - 1], (c, over_head(d), r),
            )
            for d in (2, 1, 3)
        ])

    for copy in cross_own:
        copy.wait()

    def pieces(width):
        return [slice(n * width, (n + 1) * width) for n in range(keys_b.shape[2] // width)]

    def project(t):
        here = slice(t * CHUNK, (t + 1) * CHUNK)
        for copy in row_copies[t]:
            copy.wait_recv()
        tokens = rows[:, here, :].reshape(ENTRIES * CHUNK, E)
        for cols in pieces(TILE):
            keys_raw = dot(tokens, wk_v[:, cols])
            values_b[:, here, cols] = dot(tokens, wv_v[:, cols]).astype(BF16).reshape(ENTRIES, CHUNK, TILE)
            for a in range(2):
                one = keys_raw[:, a * DH:(a + 1) * DH]
                mean = jnp.sum(one * one, axis=1, keepdims=True) * (1.0 / DH)
                factor = jnp.broadcast_to(lax.rsqrt(mean + EPSILON), one.shape)
                normed = one * factor
                at = slice(cols.start + a * DH, cols.start + (a + 1) * DH)
                factors[:, here, at] = factor.reshape(ENTRIES, CHUNK, DH)
                keys_n[:, here, at] = normed.reshape(ENTRIES, CHUNK, DH)
                keys_b[:, here, at] = normed.astype(BF16).reshape(ENTRIES, CHUNK, DH)

    for t in range(CHUNKS):
        project(t)

    lanes = lax.broadcasted_iota(jnp.int32, (SPAN, TILE), 1)

    def paired(block):
        low = jnp.where(lanes < DH, block, jnp.zeros_like(block))
        high = jnp.where(lanes >= DH, block, jnp.zeros_like(block))
        return jnp.concatenate([low, high], axis=0)

    def attend(s):
        here = slice(s * SPAN, (s + 1) * SPAN)
        mine = slice(s * NBR, (s + 1) * NBR)
        pairs = pieces(TILE)

        def span_of(array, cols):
            return array[mine, :, cols].reshape(NBR * NR, cols.stop - cols.start)

        queries = [paired(cq_v[here, cols]) for cols in pairs]
        outer = [paired(cg_v[here, cols]) for cols in pairs]
        raws = [jnp.exp(dot_nt(span_of(keys_b, cols), q) * SCALE) for cols, q in zip(pairs, queries)]
        dprobs = [dot_nt(span_of(values_b, cols), g) for cols, g in zip(pairs, outer)]
        probs = [raw * (1.0 / jnp.sum(raw, axis=0, keepdims=True)) for raw in raws]
        probs_b = [p.astype(BF16) for p in probs]
        cdeltas = [jnp.sum(p.astype(F32) * d, axis=0, keepdims=True) for p, d in zip(probs_b, dprobs)]
        dscores = [p * (d - c) for p, d, c in zip(probs, dprobs, cdeltas)]
        dscores_b = [d.astype(BF16) for d in dscores]
        grad_keys = [dot(d, q) * SCALE for d, q in zip(dscores_b, queries)]
        for cols, p, g in zip(pairs, probs_b, outer):
            value_grads[mine, :, cols] = dot(p, g).astype(BF16).reshape(NBR, NR, TILE)
        for cols, d in zip(pairs, dscores):
            part = dot(d.T.astype(BF16), span_of(keys_b, cols)) * SCALE
            cross_out[here, cols.start:cols.start + DH] = part[:SPAN, :DH].astype(BF16)
            cross_out[here, cols.start + DH:cols.stop] = part[SPAN:, DH:].astype(BF16)
        for cols, grad in zip(pairs, grad_keys):
            for a in range(2):
                at = slice(cols.start + a * DH, cols.start + (a + 1) * DH)
                one = grad[:, a * DH:(a + 1) * DH]
                normed = span_of(keys_n, at)
                mean = jnp.sum(normed * one, axis=1, keepdims=True) * (1.0 / DH)
                raw = span_of(factors, at) * (one - normed * mean)
                raw_grads[mine, :, at] = raw.astype(BF16).reshape(NBR, NR, DH)

    for s in range(2):
        attend(s)
    cross_done = keep(cross_out, ocq.at[0])

    def scatter(t):
        here = pl.ds(t * CHUNK, CHUNK)
        shape = (ENTRIES * CHUNK, keys_b.shape[2])
        term = dot_nt(raw_grads[:, here, :].reshape(shape), wk_v[...])
        term = term + dot_nt(value_grads[:, here, :].reshape(shape), wv_v[...])
        for q in range(N_HEAD):
            one = term[:, q * QUARTER:(q + 1) * QUARTER].astype(BF16)
            parts_out[q, :, here, :] = one.reshape(ENTRIES, CHUNK, QUARTER)
        return [
            send(
                parts_out.at[over_head(d), :, here], parts_in.at[h, :, here],
                s_part.at[t * 3 + d - 1], r_part.at[t * 3 + d - 1], (c, over_head(d), r),
            )
            for d in (2, 1, 3)
        ]

    part_copies = [scatter(t) for t in range(CHUNKS)]

    def share(t):
        here = pl.ds(t * CHUNK, CHUNK)
        for copy in part_copies[t]:
            copy.wait_recv()
        total = parts_out[h, :, here, :].astype(F32)
        for d in range(1, N_HEAD):
            total = total + parts_in[over_head(d), :, here, :].astype(F32)
        mine = pl.ds(r * ENTRIES, ENTRIES)
        shares[mine, here] = total.astype(BF16)
        return [
            send(
                shares.at[mine, here], shares.at[mine, here],
                s_share.at[t * 3 + d - 1], r_share.at[t * 3 + d - 1], (c, h, over_ret(d)),
            )
            for d in (2, 1, 3)
        ]

    def prepare_self():
        doc_own.wait()
        for copy in doc_copies + self_copies:
            copy.wait_recv()
        for copy in self_own:
            copy.wait()
        for b in range(N_CTX):
            one = jnp.broadcast_to(docs_v[b].astype(F32), (BLOCK, BLOCK))
            doc_cols[b * BLOCK:(b + 1) * BLOCK] = one.T

    key_at = lax.broadcasted_iota(jnp.int32, (TILE, TILE), 0)
    query_at = lax.broadcasted_iota(jnp.int32, (TILE, TILE), 1)

    def self_rows(i):
        mine = slice(i * TILE, (i + 1) * TILE)
        query, grad = held[0, mine], held[3, mine]
        query_docs = jnp.concatenate([docs_v[2 * i], docs_v[2 * i + 1]], axis=1).astype(F32)
        first = max(0, i - 2)
        totals = jnp.zeros((1, TILE), F32)
        deltas = jnp.zeros((1, TILE), F32)
        raws, dnormeds = [], []
        for j in range(first, i + 1):
            there = slice(j * TILE, (j + 1) * TILE)
            key_docs = doc_cols[there]
            visible = jnp.concatenate([key_docs, key_docs], axis=1) == query_docs
            if j == i:
                visible = visible & (key_at <= query_at)
            raw = jnp.where(visible, jnp.exp(dot_nt(held[1, there], query) * SCALE), 0.0)
            dnormed = dot_nt(held[2, there], grad)
            totals = totals + jnp.sum(raw, axis=0, keepdims=True)
            deltas = deltas + jnp.sum(raw.astype(BF16).astype(F32) * dnormed, axis=0, keepdims=True)
            raws.append(raw)
            dnormeds.append(dnormed)
        inverse = 1.0 / totals
        deltas = deltas * inverse
        query_sum = jnp.zeros((DH, TILE), F32)
        for j in range(first, i + 1):
            there = slice(j * TILE, (j + 1) * TILE)
            normed = raws[j - first] * inverse
            dscores = (normed * (dnormeds[j - first] - deltas)).astype(BF16)
            query_sum = query_sum + dot(held[1, there].astype(F32).T.astype(BF16), dscores)
            key_term = dot(dscores, query)
            value_term = dot(normed.astype(BF16), grad)
            if j == i:
                key_acc[there] = key_term
                value_acc[there] = value_term
            else:
                key_acc[there] += key_term
                value_acc[there] += value_term
        grads[0, mine] = (query_sum * SCALE).T.astype(BF16)

    def self_finish():
        grads[1] = (key_acc[...] * SCALE).astype(BF16)
        grads[2] = value_acc[...].astype(BF16)

    def self_back():
        outs = (oq, ok, ov)
        copies = []
        for d in (6, 2, 5, 3, 7, 1, 4):
            for a in range(3):
                at = (d - 1) * 3 + a
                copies.append(send(
                    grads.at[a, pl.ds(pl.multiple_of(over_ctx(d) * BLOCK, 128), BLOCK)],
                    head_of(outs[a], c),
                    s_back.at[at], r_back.at[at], (over_ctx(d), h, r),
                ))
        own = [
            keep(grads.at[a, pl.ds(pl.multiple_of(c * BLOCK, 128), BLOCK)], head_of(outs[a], c))
            for a in range(3)
        ]
        return copies, own

    prepare_self()
    self_rows(0)
    self_rows(1)
    share_copies = [share(0)]
    self_rows(2)
    share_copies.append(share(1))
    self_rows(3)
    self_finish()
    back_copies, back_own = [], []
    back_copies, back_own = self_back()

    GROUP = 16
    lane_e = lax.broadcasted_iota(jnp.int32, (1, N_RET * ENTRIES * GROUP), 1)
    named = jnp.zeros((1, N_RET * ENTRIES * GROUP), jnp.int32)
    for q in range(N_RET):
        for e in range(ENTRIES):
            k = q * ENTRIES + e
            named = jnp.where(lane_e // GROUP == k, lists_s[q, 0, e], named)
    wide = (N_HEAD * POOL_DEV * GROUP, N_RET * ENTRIES * GROUP)
    target = lax.broadcasted_iota(jnp.int32, wide, 0)
    slot = target // GROUP
    wanted = ((slot // POOL_DEV) * N_RET + r) * POOL_DEV + slot % POOL_DEV
    same_token = target % GROUP == lax.broadcasted_iota(jnp.int32, wide, 1) % GROUP
    selector = jnp.where((wanted == named) & same_token, 1.0, 0.0).astype(BF16)

    own_copies = []
    own_kept = []
    for t in range(CHUNKS):
        for copy in share_copies[t]:
            copy.wait_recv()
        for k in range(CHUNK // GROUP):
            at = slice(t * CHUNK + k * GROUP, t * CHUNK + (k + 1) * GROUP)
            stacked = shares[:, at].reshape(N_RET * ENTRIES * GROUP, QUARTER)
            summed = dot(selector, stacked)
            owned[:, at] = summed.astype(BF16).reshape(N_HEAD * POOL_DEV, GROUP, QUARTER)
        here = pl.ds(t * CHUNK, CHUNK)
        for d in (2, 1, 3):
            own_copies.append(send(
                owned.at[pl.ds(over_head(d) * POOL_DEV, POOL_DEV), here], oenc.at[:, here, my_columns],
                s_own.at[t * 3 + d - 1], r_own.at[t * 3 + d - 1], (c, over_head(d), r),
            ))
        own_kept.append(keep(owned.at[pl.ds(h * POOL_DEV, POOL_DEV), here], oenc.at[:, here, my_columns]))

    cross_done.wait()
    for copy in back_own + own_kept:
        copy.wait()
    for copy in back_copies + own_copies:
        copy.wait_recv()
    for copy in every:
        copy.wait_send()


def place_outputs(*refs):
    sources, targets, sem = refs[:5], refs[5:10], refs[10]
    copies = [pltpu.make_async_copy(sources[i], targets[i], sem.at[i]) for i in range(4)]
    for b in range(POOL_DEV):
        copies.append(pltpu.make_async_copy(sources[4].at[b], targets[4].at[b], sem.at[4 + b]))
    for copy in copies:
        copy.start()
    for copy in copies:
        copy.wait()


def on_device(
    self_query, self_key, self_value, self_grad, self_docs, cross_query, cross_grad,
    neighbours, encodings, key_weight, value_weight,
):
    block = jax.ShapeDtypeStruct(self_query.shape, BF16)
    any_space = pl.BlockSpec(memory_space=pl.ANY)
    in_specs = [pl.BlockSpec(memory_space=pltpu.HBM)] * 11
    in_specs[7] = pl.BlockSpec(memory_space=pltpu.SMEM)
    dma = pltpu.SemaphoreType.DMA
    wide = (ENTRIES, NR, key_weight.shape[1])
    scratch = [
        pltpu.VMEM((N_RET, 8, 128), jnp.int32),
        pltpu.SMEM((N_RET, 8, 128), jnp.int32),
        pltpu.VMEM((N_CTX, 1, BLOCK), jnp.int32),
        pltpu.VMEM((N_CTX * BLOCK, 128), F32),
        (pltpu.VMEM((N_HEAD * POOL_DEV, CHUNK, QUARTER), BF16),) * CHUNKS,
        pltpu.VMEM((N_RET * ENTRIES, NR, QUARTER), BF16),
        (pltpu.VMEM((N_RET * ENTRIES, CHUNK, QUARTER), BF16),) * CHUNKS,
        pltpu.VMEM((ENTRIES, NR, E), BF16),
        pltpu.VMEM((4, N_CTX * BLOCK, DH), BF16),
        pltpu.VMEM((N_CTX * BLOCK, DH), F32),
        pltpu.VMEM((N_CTX * BLOCK, DH), F32),
        pltpu.VMEM((3, N_CTX * BLOCK, DH), BF16),
        pltpu.VMEM(key_weight.shape, BF16),
        pltpu.VMEM(value_weight.shape, BF16),
        pltpu.VMEM(cross_query.shape[1:], BF16),
        pltpu.VMEM(cross_grad.shape[1:], BF16),
        pltpu.VMEM(cross_grad.shape[1:], BF16),
        pltpu.VMEM(wide, F32),
        pltpu.VMEM(wide, F32),
        pltpu.VMEM(wide, BF16),
        pltpu.VMEM(wide, BF16),
        pltpu.VMEM(wide, BF16),
        pltpu.VMEM(wide, BF16),
        pltpu.VMEM((N_HEAD, ENTRIES, NR, QUARTER), BF16),
        pltpu.VMEM((N_HEAD, ENTRIES, NR, QUARTER), BF16),
        pltpu.VMEM((N_RET * ENTRIES, NR, QUARTER), BF16),
        pltpu.VMEM((N_HEAD * POOL_DEV, NR, QUARTER), BF16),
        dma((24,)),
        dma((3,)), dma((3,)),
        dma((7,)), dma((7,)),
        dma((3 * CHUNKS,)), dma((3 * CHUNKS,)),
        dma((3 * CHUNKS,)), dma((3 * CHUNKS,)),
        dma((3 * CHUNKS,)), dma((3 * CHUNKS,)),
        dma((28,)), dma((28,)),
        dma((3 * CHUNKS,)), dma((3 * CHUNKS,)),
        dma((3 * CHUNKS,)), dma((3 * CHUNKS,)),
        dma((3 * CHUNKS,)), dma((3 * CHUNKS,)),
        dma((21,)), dma((21,)),
    ]
    outs = pl.pallas_call(
        kernel,
        out_shape=(block, block, block, block, jax.ShapeDtypeStruct(encodings.shape, BF16)),
        in_specs=in_specs,
        out_specs=(any_space,) * 5,
        scratch_shapes=scratch,
        compiler_params=pltpu.CompilerParams(
            collective_id=0, has_side_effects=True, vmem_limit_bytes=32 * 2**20
        ),
        name="retro_backward",
    )(*[
        pltpu.with_memory_space_constraint(array, pltpu.HBM)
        for array in (self_query, self_key, self_value, self_grad, self_docs, cross_query, cross_grad)
    ], pltpu.with_memory_space_constraint(neighbours, pltpu.SMEM), *[
        pltpu.with_memory_space_constraint(array, pltpu.HBM)
        for array in (encodings, key_weight, value_weight)
    ])
    return pl.pallas_call(
        place_outputs,
        out_shape=(block, block, block, block, jax.ShapeDtypeStruct(encodings.shape, BF16)),
        in_specs=[any_space] * 5,
        out_specs=(pl.BlockSpec(memory_space=pltpu.HBM),) * 5,
        scratch_shapes=[dma((4 + POOL_DEV,))],
        name="place_outputs",
    )(*[pltpu.with_memory_space_constraint(out, pltpu.VMEM) for out in outs])


def solution(mesh):
    tokens = P("ret", "ctx", "head")
    pool = P(("ctx", "head", "ret"), None, None)
    placed = (
        tokens, tokens, tokens, tokens, P("ret", "ctx"), tokens, tokens,
        P("ret", "ctx", None), pool, P(None, "head"), P(None, "head"),
    )
    return jax.shard_map(
        on_device,
        mesh=mesh,
        in_specs=placed,
        out_specs=(tokens, tokens, tokens, tokens, pool),
        check_vma=False,
    )
```

```python
import functools
import math

import jax
import jax.numpy as jnp
from jax import lax
from jax.experimental import pallas as pl
from jax.experimental.pallas import tpu as pltpu
from jax.sharding import PartitionSpec as P

SPAN = 64
NBR = 2
NR = 128
E = 512
DH = 128
POOL_DEV = 8
EPSILON = 1e-06
SCALE = 1.0 / math.sqrt(DH)

N_CTX = 8
N_HEAD = 4
N_RET = 4
ENTRIES = 4
BLOCK = 128
TILE = 256
QUARTER = E // N_HEAD
CHUNKS = 4
ORDER_BACK = (4, 5, 7, 6, 1, 3, 2)
CHUNK = NR // CHUNKS

MESH = pl.DeviceIdType.MESH
F32 = jnp.float32
BF16 = jnp.bfloat16


def dot(a, b):
    return lax.dot_general(a, b, (((1,), (0,)), ((), ())), preferred_element_type=F32)


def dot_nt(a, b):
    return lax.dot_general(a, b, (((1,), (1,)), ((), ())), preferred_element_type=F32)


def kernel(
    sq, sk, sv, sg, docs, cq, cg, nbr, enc, wk, wv,
    oq, ok, ov, ocq, oenc,
    nbr_s, lists_v, lists_s, docs_v, doc_cols, pool, outgoing, incoming, rows, held, key_acc, value_acc, grads,
    wk_v, wv_v, cq_v, cg_v, cross_out, keys_n, factors, keys_b, values_b, raw_grads, value_grads, parts_out, parts_in, shares, owned, selector,
    loc, s_list, r_list, s_docs, r_docs, s_pool, r_pool, s_ret, r_ret, s_rows, r_rows, s_self, r_self,
    s_part, r_part, s_share, r_share, s_own, r_own, s_back, r_back,
):
    c, h, r = lax.axis_index("ctx"), lax.axis_index("head"), lax.axis_index("ret")

    def over_ctx(d):
        return lax.rem(c + d, N_CTX)

    def ctx_peer(d):
        far, step = divmod(d, 4)
        half = lax.rem(lax.div(c, 4) + far, 2)
        return half * 4 + lax.rem(lax.rem(c, 4) + step, 4)

    def over_head(d):
        return lax.rem(h + d, N_HEAD)

    def over_ret(d):
        return lax.rem(r + d, N_RET)

    def send(src, dst, ssem, rsem, device):
        copy = pltpu.make_async_remote_copy(
            src_ref=src, dst_ref=dst, send_sem=ssem, recv_sem=rsem,
            device_id=device, device_id_type=MESH,
        )
        copy.start()
        every.append(copy)
        return copy

    every = []
    local_count = [0]

    def keep(src, dst):
        copy = pltpu.make_async_copy(src, dst, loc.at[local_count[0]])
        local_count[0] += 1
        copy.start()
        return copy

    wanted_copy = keep(nbr, nbr_s)
    barrier = pltpu.get_barrier_semaphore()
    peers = [(over_ctx(d), h, r) for d in range(1, N_CTX)]
    peers += [(c, over_head(d), r) for d in range(1, N_HEAD)]
    peers += [(c, h, over_ret(d)) for d in range(1, N_RET)]
    for peer in peers:
        pl.semaphore_signal(barrier, inc=1, device_id=peer, device_id_type=MESH)
    wanted_copy.wait()
    lane = lax.broadcasted_iota(jnp.int32, (8, 128), 1)
    tile = jnp.zeros((8, 128), jnp.int32)
    for e in range(ENTRIES):
        tile = jnp.where(lane == e, nbr_s[0, e // NBR, e % NBR], tile)
    lists_v[r] = tile
    pl.semaphore_wait(barrier, len(peers))

    def quarter_of(owner_column, t):
        return enc.at[:, pl.ds(t * CHUNK, CHUNK), pl.ds(pl.multiple_of(owner_column * QUARTER, 128), QUARTER)]

    pool_copies = []
    pool_own = []
    for t in range(CHUNKS):
        pool_copies.append([
            send(
                quarter_of(over_head(d), t),
                pool[t].at[pl.ds(h * POOL_DEV, POOL_DEV)],
                s_pool.at[t * 3 + d - 1], r_pool.at[t * 3 + d - 1], (c, over_head(d), r),
            )
            for d in (1, 3, 2)
        ])
        if t == 0:
            list_copies = [
                send(lists_v.at[r], lists_v.at[r], s_list.at[d - 1], r_list.at[d - 1], (c, h, over_ret(d)))
                for d in range(1, N_RET)
            ]
    for t in range(CHUNKS):
        pool_own.append(
            keep(quarter_of(h, t), pool[t].at[pl.ds(h * POOL_DEV, POOL_DEV)])
        )
    doc_copies = [
        send(docs, docs_v.at[c], s_docs.at[d - 1], r_docs.at[d - 1], (over_ctx(d), h, r))
        for d in range(1, N_CTX)
    ]
    doc_own = keep(docs, docs_v.at[c])
    self_in = (sq, sk, sv, sg)

    def head_of(array, number):
        return array.at[0, :, pl.ds(pl.multiple_of(number * DH, 128), DH)]

    self_copies = []
    self_own = []

    def self_start(order):
        for d in order:
            for a in range(4):
                at = (d - 1) * 4 + a
                self_copies.append(send(
                    head_of(self_in[a], ctx_peer(d)),
                    held.at[a, pl.ds(pl.multiple_of(c * BLOCK, 128), BLOCK)],
                    s_self.at[at], r_self.at[at], (ctx_peer(d), h, r),
                ))

    def self_keep():
        for a in range(4):
            self_own.append(
                keep(head_of(self_in[a], c), held.at[a, pl.ds(pl.multiple_of(c * BLOCK, 128), BLOCK)])
            )

    self_start((1, 3, 2))
    self_keep()
    cross_own = [keep(wk, wk_v), keep(wv, wv_v), keep(cq.at[0], cq_v), keep(cg.at[0], cg_v)]

    for copy in list_copies:
        copy.wait_recv()
    to_scalars = keep(lists_v, lists_s)
    to_scalars.wait()

    ret_copies = []
    row_copies = []
    my_columns = pl.ds(pl.multiple_of(h * QUARTER, 128), QUARTER)

    def hand_out(t):
        here = pl.ds(t * CHUNK, CHUNK)
        pool_own[t].wait()
        for copy in pool_copies[t]:
            copy.wait_recv()
        for q in range(N_RET):
            for e in range(ENTRIES):
                value = lists_s[q, 0, e]
                place = lax.div(value, N_RET * POOL_DEV) * POOL_DEV + lax.rem(value, POOL_DEV)
                outgoing[q * ENTRIES + e, here] = pool[t][place]
        ret_copies.append([
            send(
                outgoing.at[pl.ds(over_ret(d) * ENTRIES, ENTRIES), here],
                incoming[t].at[pl.ds(r * ENTRIES, ENTRIES)],
                s_ret.at[t * 3 + d - 1], r_ret.at[t * 3 + d - 1], (c, h, over_ret(d)),
            )
            for d in (1, 3, 2)
        ])
        incoming[t][pl.ds(r * ENTRIES, ENTRIES)] = outgoing[pl.ds(r * ENTRIES, ENTRIES), here]

    def spread(t):
        here = pl.ds(t * CHUNK, CHUNK)
        for copy in ret_copies[t]:
            copy.wait_recv()
        for e in range(ENTRIES):
            value = lists_s[r, 0, e]
            column = lax.rem(lax.div(value, POOL_DEV), N_RET)
            rows[e, here, my_columns] = incoming[t][column * ENTRIES + e]
        row_copies.append([
            send(
                rows.at[:, here, my_columns], rows.at[:, here, my_columns],
                s_rows.at[t * 3 + d - 1], r_rows.at[t * 3 + d - 1], (c, over_head(d), r),
            )
            for d in (1, 3, 2)
        ])

    for t in range(CHUNKS + 1):
        if t < CHUNKS:
            hand_out(t)
        if t == CHUNKS - 1:
            self_start((4, 5, 7, 6))
        if t >= 1:
            spread(t - 1)

    GROUP = 16
    lane_e = lax.broadcasted_iota(jnp.int32, (1, N_RET * ENTRIES * GROUP), 1)
    named = jnp.zeros((1, N_RET * ENTRIES * GROUP), jnp.int32)
    for q in range(N_RET):
        for e in range(ENTRIES):
            k = q * ENTRIES + e
            named = jnp.where(lane_e // GROUP == k, lists_s[q, 0, e], named)
    wide = (N_HEAD * POOL_DEV * GROUP, N_RET * ENTRIES * GROUP)
    target = lax.broadcasted_iota(jnp.int32, wide, 0)
    slot = target // GROUP
    wanted = ((slot // POOL_DEV) * N_RET + r) * POOL_DEV + slot % POOL_DEV
    same_token = target % GROUP == lax.broadcasted_iota(jnp.int32, wide, 1) % GROUP
    selector[...] = jnp.where((wanted == named) & same_token, 1.0, 0.0).astype(BF16)

    def prepare_self():
        doc_own.wait()
        for copy in doc_copies + self_copies:
            copy.wait_recv()
        for copy in self_own:
            copy.wait()
        for b in range(N_CTX):
            one = jnp.broadcast_to(docs_v[b].astype(F32), (BLOCK, BLOCK))
            doc_cols[b * BLOCK:(b + 1) * BLOCK] = one.T

    key_at = lax.broadcasted_iota(jnp.int32, (TILE, TILE), 0)
    query_at = lax.broadcasted_iota(jnp.int32, (TILE, TILE), 1)

    def self_rows(i):
        mine = slice(i * TILE, (i + 1) * TILE)
        query, grad = held[0, mine], held[3, mine]
        query_docs = jnp.concatenate([docs_v[2 * i], docs_v[2 * i + 1]], axis=1).astype(F32)
        first = max(0, i - 2)
        totals = jnp.zeros((1, TILE), F32)
        deltas = jnp.zeros((1, TILE), F32)
        raws, dnormeds = [], []
        for j in range(first, i + 1):
            there = slice(j * TILE, (j + 1) * TILE)
            key_docs = doc_cols[there]
            visible = jnp.concatenate([key_docs, key_docs], axis=1) == query_docs
            if j == i:
                visible = visible & (key_at <= query_at)
            raw = jnp.where(visible, jnp.exp(dot_nt(held[1, there], query) * SCALE), 0.0)
            dnormed = dot_nt(held[2, there], grad)
            totals = totals + jnp.sum(raw, axis=0, keepdims=True)
            deltas = deltas + jnp.sum(raw.astype(BF16).astype(F32) * dnormed, axis=0, keepdims=True)
            raws.append(raw)
            dnormeds.append(dnormed)
        inverse = 1.0 / totals
        deltas = deltas * inverse
        query_sum = jnp.zeros((DH, TILE), F32)
        for j in range(first, i + 1):
            there = slice(j * TILE, (j + 1) * TILE)
            normed = raws[j - first] * inverse
            dscores = (normed * (dnormeds[j - first] - deltas)).astype(BF16)
            query_sum = query_sum + dot(held[1, there].astype(F32).T.astype(BF16), dscores)
            key_term = dot(dscores, query)
            value_term = dot(normed.astype(BF16), grad)
            if j == i:
                key_acc[there] = key_term
                value_acc[there] = value_term
            else:
                key_acc[there] += key_term
                value_acc[there] += value_term
        grads[0, mine] = (query_sum * SCALE).T.astype(BF16)

    def self_finish():
        grads[1] = (key_acc[...] * SCALE).astype(BF16)
        grads[2] = value_acc[...].astype(BF16)

    def self_back():
        outs = (oq, ok, ov)
        copies = []
        for d in ORDER_BACK:
            for a in range(3):
                at = (d - 1) * 3 + a
                copies.append(send(
                    grads.at[a, pl.ds(pl.multiple_of(ctx_peer(d) * BLOCK, 128), BLOCK)],
                    head_of(outs[a], c),
                    s_back.at[at], r_back.at[at], (ctx_peer(d), h, r),
                ))
        own = [
            keep(grads.at[a, pl.ds(pl.multiple_of(c * BLOCK, 128), BLOCK)], head_of(outs[a], c))
            for a in range(3)
        ]
        return copies, own

    for copy in cross_own:
        copy.wait()

    def pieces(width):
        return [slice(n * width, (n + 1) * width) for n in range(keys_b.shape[2] // width)]

    def project(t):
        here = slice(t * CHUNK, (t + 1) * CHUNK)
        for copy in row_copies[t]:
            copy.wait_recv()
        tokens = rows[:, here, :].reshape(ENTRIES * CHUNK, E)
        for cols in pieces(TILE):
            keys_raw = dot(tokens, wk_v[:, cols])
            values_b[:, here, cols] = dot(tokens, wv_v[:, cols]).astype(BF16).reshape(ENTRIES, CHUNK, TILE)
            for a in range(2):
                one = keys_raw[:, a * DH:(a + 1) * DH]
                mean = jnp.sum(one * one, axis=1, keepdims=True) * (1.0 / DH)
                factor = jnp.broadcast_to(lax.rsqrt(mean + EPSILON), one.shape)
                normed = one * factor
                at = slice(cols.start + a * DH, cols.start + (a + 1) * DH)
                factors[:, here, at] = factor.reshape(ENTRIES, CHUNK, DH)
                keys_n[:, here, at] = normed.reshape(ENTRIES, CHUNK, DH)
                keys_b[:, here, at] = normed.astype(BF16).reshape(ENTRIES, CHUNK, DH)

    for t in range(CHUNKS):
        project(t)

    lanes = lax.broadcasted_iota(jnp.int32, (SPAN, TILE), 1)

    def paired(block):
        low = jnp.where(lanes < DH, block, jnp.zeros_like(block))
        high = jnp.where(lanes >= DH, block, jnp.zeros_like(block))
        return jnp.concatenate([low, high], axis=0)

    def attend(s):
        here = slice(s * SPAN, (s + 1) * SPAN)
        mine = slice(s * NBR, (s + 1) * NBR)
        pairs = pieces(TILE)

        def span_of(array, cols):
            return array[mine, :, cols].reshape(NBR * NR, cols.stop - cols.start)

        queries = [paired(cq_v[here, cols]) for cols in pairs]
        outer = [paired(cg_v[here, cols]) for cols in pairs]
        raws = [jnp.exp(dot_nt(span_of(keys_b, cols), q) * SCALE) for cols, q in zip(pairs, queries)]
        dprobs = [dot_nt(span_of(values_b, cols), g) for cols, g in zip(pairs, outer)]
        probs = [raw * (1.0 / jnp.sum(raw, axis=0, keepdims=True)) for raw in raws]
        probs_b = [p.astype(BF16) for p in probs]
        cdeltas = [jnp.sum(p.astype(F32) * d, axis=0, keepdims=True) for p, d in zip(probs_b, dprobs)]
        dscores = [p * (d - c) for p, d, c in zip(probs, dprobs, cdeltas)]
        dscores_b = [d.astype(BF16) for d in dscores]
        grad_keys = [dot(d, q) * SCALE for d, q in zip(dscores_b, queries)]
        for cols, p, g in zip(pairs, probs_b, outer):
            value_grads[mine, :, cols] = dot(p, g).astype(BF16).reshape(NBR, NR, TILE)
        for cols, d in zip(pairs, dscores):
            part = dot(d.T.astype(BF16), span_of(keys_b, cols)) * SCALE
            cross_out[here, cols.start:cols.start + DH] = part[:SPAN, :DH].astype(BF16)
            cross_out[here, cols.start + DH:cols.stop] = part[SPAN:, DH:].astype(BF16)
        for cols, grad in zip(pairs, grad_keys):
            for a in range(2):
                at = slice(cols.start + a * DH, cols.start + (a + 1) * DH)
                one = grad[:, a * DH:(a + 1) * DH]
                normed = span_of(keys_n, at)
                mean = jnp.sum(normed * one, axis=1, keepdims=True) * (1.0 / DH)
                raw = span_of(factors, at) * (one - normed * mean)
                raw_grads[mine, :, at] = raw.astype(BF16).reshape(NBR, NR, DH)

    for s in range(2):
        attend(s)
    cross_done = keep(cross_out, ocq.at[0])

    def scatter(t):
        here = pl.ds(t * CHUNK, CHUNK)
        shape = (ENTRIES * CHUNK, keys_b.shape[2])
        term = dot_nt(raw_grads[:, here, :].reshape(shape), wk_v[...])
        term = term + dot_nt(value_grads[:, here, :].reshape(shape), wv_v[...])
        for q in range(N_HEAD):
            one = term[:, q * QUARTER:(q + 1) * QUARTER].astype(BF16)
            parts_out[q, :, here, :] = one.reshape(ENTRIES, CHUNK, QUARTER)
        return [
            send(
                parts_out.at[over_head(d), :, here], parts_in.at[h, :, here],
                s_part.at[t * 3 + d - 1], r_part.at[t * 3 + d - 1], (c, over_head(d), r),
            )
            for d in (1, 3, 2)
        ]

    part_copies = [scatter(t) for t in range(CHUNKS)]

    def share(t):
        here = pl.ds(t * CHUNK, CHUNK)
        for copy in part_copies[t]:
            copy.wait_recv()
        total = parts_out[h, :, here, :].astype(F32)
        for d in range(1, N_HEAD):
            total = total + parts_in[over_head(d), :, here, :].astype(F32)
        mine = pl.ds(r * ENTRIES, ENTRIES)
        shares[mine, here] = total.astype(BF16)
        return [
            send(
                shares.at[mine, here], shares.at[mine, here],
                s_share.at[t * 3 + d - 1], r_share.at[t * 3 + d - 1], (c, h, over_ret(d)),
            )
            for d in (1, 3, 2)
        ]

    own_copies = []
    own_kept = []

    def hand_back(t):
        for copy in share_copies[t]:
            copy.wait_recv()
        for k in range(CHUNK // GROUP):
            at = slice(t * CHUNK + k * GROUP, t * CHUNK + (k + 1) * GROUP)
            stacked = shares[:, at].reshape(N_RET * ENTRIES * GROUP, QUARTER)
            summed = dot(selector[...], stacked)
            owned[:, at] = summed.astype(BF16).reshape(N_HEAD * POOL_DEV, GROUP, QUARTER)
        here = pl.ds(t * CHUNK, CHUNK)
        for d in (1, 3, 2):
            own_copies.append(send(
                owned.at[pl.ds(over_head(d) * POOL_DEV, POOL_DEV), here], oenc.at[:, here, my_columns],
                s_own.at[t * 3 + d - 1], r_own.at[t * 3 + d - 1], (c, over_head(d), r),
            ))
        own_kept.append(keep(owned.at[pl.ds(h * POOL_DEV, POOL_DEV), here], oenc.at[:, here, my_columns]))

    back_copies, back_own = [], []
    share_copies = []
    prepare_self()
    self_rows(0)
    self_rows(1)
    share_copies.append(share(0))
    share_copies.append(share(1))
    self_rows(2)
    share_copies.append(share(2))
    share_copies.append(share(3))
    hand_back(0)
    self_rows(3)
    self_finish()
    hand_back(1)
    back_copies, back_own = self_back()
    hand_back(2)
    hand_back(3)

    cross_done.wait()
    for copy in back_own + own_kept:
        copy.wait()
    for copy in back_copies + own_copies:
        copy.wait_recv()
    for copy in every:
        copy.wait_send()


def place_outputs(*refs):
    sources, targets, sem = refs[:5], refs[5:10], refs[10]
    copies = [pltpu.make_async_copy(sources[i], targets[i], sem.at[i]) for i in range(4)]
    for b in range(POOL_DEV):
        copies.append(pltpu.make_async_copy(sources[4].at[b], targets[4].at[b], sem.at[4 + b]))
    for copy in copies:
        copy.start()
    for copy in copies:
        copy.wait()


def on_device(
    self_query, self_key, self_value, self_grad, self_docs, cross_query, cross_grad,
    neighbours, encodings, key_weight, value_weight,
):
    block = jax.ShapeDtypeStruct(self_query.shape, BF16)
    any_space = pl.BlockSpec(memory_space=pl.ANY)
    in_specs = [pl.BlockSpec(memory_space=pltpu.HBM)] * 11
    dma = pltpu.SemaphoreType.DMA
    wide = (ENTRIES, NR, key_weight.shape[1])
    scratch = [
        pltpu.SMEM(neighbours.shape, jnp.int32),
        pltpu.VMEM((N_RET, 8, 128), jnp.int32),
        pltpu.SMEM((N_RET, 8, 128), jnp.int32),
        pltpu.VMEM((N_CTX, 1, BLOCK), jnp.int32),
        pltpu.VMEM((N_CTX * BLOCK, 128), F32),
        (pltpu.VMEM((N_HEAD * POOL_DEV, CHUNK, QUARTER), BF16),) * CHUNKS,
        pltpu.VMEM((N_RET * ENTRIES, NR, QUARTER), BF16),
        (pltpu.VMEM((N_RET * ENTRIES, CHUNK, QUARTER), BF16),) * CHUNKS,
        pltpu.VMEM((ENTRIES, NR, E), BF16),
        pltpu.VMEM((4, N_CTX * BLOCK, DH), BF16),
        pltpu.VMEM((N_CTX * BLOCK, DH), F32),
        pltpu.VMEM((N_CTX * BLOCK, DH), F32),
        pltpu.VMEM((3, N_CTX * BLOCK, DH), BF16),
        pltpu.VMEM(key_weight.shape, BF16),
        pltpu.VMEM(value_weight.shape, BF16),
        pltpu.VMEM(cross_query.shape[1:], BF16),
        pltpu.VMEM(cross_grad.shape[1:], BF16),
        pltpu.VMEM(cross_grad.shape[1:], BF16),
        pltpu.VMEM(wide, F32),
        pltpu.VMEM(wide, F32),
        pltpu.VMEM(wide, BF16),
        pltpu.VMEM(wide, BF16),
        pltpu.VMEM(wide, BF16),
        pltpu.VMEM(wide, BF16),
        pltpu.VMEM((N_HEAD, ENTRIES, NR, QUARTER), BF16),
        pltpu.VMEM((N_HEAD, ENTRIES, NR, QUARTER), BF16),
        pltpu.VMEM((N_RET * ENTRIES, NR, QUARTER), BF16),
        pltpu.VMEM((N_HEAD * POOL_DEV, NR, QUARTER), BF16),
        pltpu.VMEM((N_HEAD * POOL_DEV * 16, N_RET * ENTRIES * 16), BF16),
        dma((32,)),
        dma((3,)), dma((3,)),
        dma((7,)), dma((7,)),
        dma((3 * CHUNKS,)), dma((3 * CHUNKS,)),
        dma((3 * CHUNKS,)), dma((3 * CHUNKS,)),
        dma((3 * CHUNKS,)), dma((3 * CHUNKS,)),
        dma((28,)), dma((28,)),
        dma((3 * CHUNKS,)), dma((3 * CHUNKS,)),
        dma((3 * CHUNKS,)), dma((3 * CHUNKS,)),
        dma((3 * CHUNKS,)), dma((3 * CHUNKS,)),
        dma((21,)), dma((21,)),
    ]
    outs = pl.pallas_call(
        kernel,
        out_shape=(block, block, block, block, jax.ShapeDtypeStruct(encodings.shape, BF16)),
        in_specs=in_specs,
        out_specs=(any_space,) * 5,
        scratch_shapes=scratch,
        compiler_params=pltpu.CompilerParams(
            collective_id=0, has_side_effects=True, vmem_limit_bytes=32 * 2**20
        ),
        name="retro_backward",
    )(*[
        pltpu.with_memory_space_constraint(array, pltpu.HBM)
        for array in (self_query, self_key, self_value, self_grad, self_docs, cross_query, cross_grad)
    ], pltpu.with_memory_space_constraint(neighbours, pltpu.HBM), *[
        pltpu.with_memory_space_constraint(array, pltpu.HBM)
        for array in (encodings, key_weight, value_weight)
    ])
    return pl.pallas_call(
        place_outputs,
        out_shape=(block, block, block, block, jax.ShapeDtypeStruct(encodings.shape, BF16)),
        in_specs=[any_space] * 5,
        out_specs=(pl.BlockSpec(memory_space=pltpu.HBM),) * 5,
        scratch_shapes=[dma((4 + POOL_DEV,))],
        name="place_outputs",
    )(*[pltpu.with_memory_space_constraint(out, pltpu.VMEM) for out in outs])


def solution(mesh):
    tokens = P("ret", "ctx", "head")
    pool = P(("ctx", "head", "ret"), None, None)
    placed = (
        tokens, tokens, tokens, tokens, P("ret", "ctx"), tokens, tokens,
        P("ret", "ctx", None), pool, P(None, "head"), P(None, "head"),
    )
    return jax.shard_map(
        on_device,
        mesh=mesh,
        in_specs=placed,
        out_specs=(tokens, tokens, tokens, tokens, pool),
        check_vma=False,
    )
```

```python
import functools
import math

import jax
import jax.numpy as jnp
from jax import lax
from jax.experimental import pallas as pl
from jax.experimental.pallas import tpu as pltpu
from jax.sharding import PartitionSpec as P

SPAN = 64
NBR = 2
NR = 128
E = 512
DH = 128
POOL_DEV = 8
EPSILON = 1e-06
SCALE = 1.0 / math.sqrt(DH)

N_CTX = 8
N_HEAD = 4
N_RET = 4
ENTRIES = 4
BLOCK = 128
TILE = 256
DOC_ROWS = 16
QUARTER = E // N_HEAD
CHUNKS = 4
ORDER_BACK = (4, 5, 7, 6, 1, 3, 2)
CHUNK = NR // CHUNKS

MESH = pl.DeviceIdType.MESH
F32 = jnp.float32
BF16 = jnp.bfloat16


def dot(a, b):
    return lax.dot_general(a, b, (((1,), (0,)), ((), ())), preferred_element_type=F32)


def dot_nt(a, b):
    return lax.dot_general(a, b, (((1,), (1,)), ((), ())), preferred_element_type=F32)


def kernel(
    sq, sk, sv, sg, docs, cq, cg, nbr, enc, wk, wv,
    oself, ocq, oenc,
    nbr_s, lists_v, lists_s, docs_v, doc_cols, staged, pool, outgoing, incoming, rows, held, key_acc, value_acc, grads,
    wk_v, wv_v, cq_v, cg_v, cross_out, keys_n, factors, keys_b, values_b, raw_grads, value_grads, parts_out, parts_in, shares, owned, selector,
    loc, s_list, r_list, s_pool, r_pool, s_ret, r_ret, s_rows, r_rows, s_self, r_self,
    s_part, r_part, s_share, r_share, s_own, r_own, s_back, r_back,
):
    c, h, r = lax.axis_index("ctx"), lax.axis_index("head"), lax.axis_index("ret")

    def over_ctx(d):
        return lax.rem(c + d, N_CTX)

    def ctx_peer(d):
        far, step = divmod(d, 4)
        half = lax.rem(lax.div(c, 4) + far, 2)
        return half * 4 + lax.rem(lax.rem(c, 4) + step, 4)

    def over_head(d):
        return lax.rem(h + d, N_HEAD)

    def over_ret(d):
        return lax.rem(r + d, N_RET)

    def send(src, dst, ssem, rsem, device):
        copy = pltpu.make_async_remote_copy(
            src_ref=src, dst_ref=dst, send_sem=ssem, recv_sem=rsem,
            device_id=device, device_id_type=MESH,
        )
        copy.start()
        every.append(copy)
        return copy

    every = []

    def flush(left):
        while len(every) > left:
            every.pop(0).wait_send()

    local_count = [0]

    def keep(src, dst):
        copy = pltpu.make_async_copy(src, dst, loc.at[local_count[0]])
        local_count[0] += 1
        copy.start()
        return copy

    wanted_copy = keep(nbr, nbr_s)
    doc_copy = keep(docs, docs_v)
    staging = [
        keep(array.at[0], staged.at[pl.ds(a * BLOCK, BLOCK)]) for a, array in enumerate((sq, sk, sv, sg))
    ]
    barrier = pltpu.get_barrier_semaphore()
    peers = [(over_ctx(d), h, r) for d in range(1, N_CTX)]
    peers += [(c, over_head(d), r) for d in range(1, N_HEAD)]
    peers += [(c, h, over_ret(d)) for d in range(1, N_RET)]
    for peer in peers:
        pl.semaphore_signal(barrier, inc=1, device_id=peer, device_id_type=MESH)
    wanted_copy.wait()
    lane = lax.broadcasted_iota(jnp.int32, (8, 128), 1)
    tile = jnp.zeros((8, 128), jnp.int32)
    for e in range(ENTRIES):
        tile = jnp.where(lane == e, nbr_s[0, e // NBR, e % NBR], tile)
    lists_v[r] = tile
    doc_copy.wait()
    doc_rows = jnp.broadcast_to(docs_v[...].astype(F32), (DOC_ROWS, BLOCK)).astype(BF16)
    for k in range(N_CTX):
        staged[4 * BLOCK:, k * DH:(k + 1) * DH] = doc_rows
    pl.semaphore_wait(barrier, len(peers))

    def quarter_of(owner_column, t):
        return enc.at[:, pl.ds(t * CHUNK, CHUNK), pl.ds(pl.multiple_of(owner_column * QUARTER, 128), QUARTER)]

    pool_copies = []
    pool_own = []
    for t in range(CHUNKS):
        pool_copies.append([
            send(
                quarter_of(over_head(d), t),
                pool[t].at[pl.ds(h * POOL_DEV, POOL_DEV)],
                s_pool.at[t * 3 + d - 1], r_pool.at[t * 3 + d - 1], (c, over_head(d), r),
            )
            for d in (1, 3, 2)
        ])
        if t == 0:
            list_copies = [
                send(lists_v.at[r], lists_v.at[r], s_list.at[d - 1], r_list.at[d - 1], (c, h, over_ret(d)))
                for d in range(1, N_RET)
            ]
    for t in range(CHUNKS):
        pool_own.append(
            keep(quarter_of(h, t), pool[t].at[pl.ds(h * POOL_DEV, POOL_DEV)])
        )
    self_copies = []
    self_own = []

    def head_columns(number):
        return pl.ds(pl.multiple_of(number * DH, 128), DH)

    def self_start(order):
        for d in order:
            self_copies.append(send(
                staged.at[:, head_columns(ctx_peer(d))], held.at[c],
                s_self.at[d - 1], r_self.at[d - 1], (ctx_peer(d), h, r),
            ))

    for copy in staging:
        copy.wait()
    self_start((1, 3, 2))
    self_own.append(keep(staged.at[:, head_columns(c)], held.at[c]))
    cross_own = [keep(wk, wk_v), keep(wv, wv_v), keep(cq.at[0], cq_v), keep(cg.at[0], cg_v)]

    for copy in list_copies:
        copy.wait_recv()
    to_scalars = keep(lists_v, lists_s)
    to_scalars.wait()

    entries = [[lists_s[q, 0, e] for e in range(ENTRIES)] for q in range(N_RET)]
    places = [[(v >> 5) * POOL_DEV + (v & 7) for v in one] for one in entries]
    wanted_columns = [(lists_s[r, 0, e] >> 3) & 3 for e in range(ENTRIES)]
    ret_copies = []
    row_copies = []
    my_columns = pl.ds(pl.multiple_of(h * QUARTER, 128), QUARTER)

    def hand_out(t):
        here = pl.ds(t * CHUNK, CHUNK)
        pool_own[t].wait()
        for copy in pool_copies[t]:
            copy.wait_recv()
        for q in range(N_RET):
            for e in range(ENTRIES):
                outgoing[q * ENTRIES + e, here] = pool[t][places[q][e]]
        ret_copies.append([
            send(
                outgoing.at[pl.ds(over_ret(d) * ENTRIES, ENTRIES), here],
                incoming[t].at[pl.ds(r * ENTRIES, ENTRIES)],
                s_ret.at[t * 3 + d - 1], r_ret.at[t * 3 + d - 1], (c, h, over_ret(d)),
            )
            for d in (1, 3, 2)
        ])
        incoming[t][pl.ds(r * ENTRIES, ENTRIES)] = outgoing[pl.ds(r * ENTRIES, ENTRIES), here]

    def spread(t):
        here = pl.ds(t * CHUNK, CHUNK)
        for copy in ret_copies[t]:
            copy.wait_recv()
        for e in range(ENTRIES):
            rows[e, here, my_columns] = incoming[t][wanted_columns[e] * ENTRIES + e]
        row_copies.append([
            send(
                rows.at[:, here, my_columns], rows.at[:, here, my_columns],
                s_rows.at[t * 3 + d - 1], r_rows.at[t * 3 + d - 1], (c, over_head(d), r),
            )
            for d in (1, 3, 2)
        ])

    for t in range(CHUNKS + 1):
        if t < CHUNKS:
            hand_out(t)
        if t == CHUNKS - 1:
            self_start((4, 5, 7, 6))
        if t >= 1:
            spread(t - 1)

    GROUP = 16
    lane_e = lax.broadcasted_iota(jnp.int32, (1, N_RET * ENTRIES * GROUP), 1)
    named = jnp.zeros((1, N_RET * ENTRIES * GROUP), jnp.int32)
    for q in range(N_RET):
        for e in range(ENTRIES):
            k = q * ENTRIES + e
            named = jnp.where(lane_e // GROUP == k, entries[q][e], named)
    wide = (N_HEAD * POOL_DEV * GROUP, N_RET * ENTRIES * GROUP)
    target = lax.broadcasted_iota(jnp.int32, wide, 0)
    slot = target // GROUP
    wanted = ((slot // POOL_DEV) * N_RET + r) * POOL_DEV + slot % POOL_DEV
    same_token = target % GROUP == lax.broadcasted_iota(jnp.int32, wide, 1) % GROUP
    selector[...] = jnp.where((wanted == named) & same_token, 1.0, 0.0).astype(BF16)

    def doc_row(b):
        return held[b, 4 * BLOCK:, :].astype(F32)[:1]

    def tokens_of(a, i):
        return held[2 * i:2 * i + 2, a * BLOCK:(a + 1) * BLOCK, :].reshape(TILE, DH)

    def prepare_self():
        for copy in self_copies:
            copy.wait_recv()
        for copy in self_own:
            copy.wait()
        for b in range(N_CTX):
            one = jnp.broadcast_to(doc_row(b), (BLOCK, BLOCK))
            doc_cols[b * BLOCK:(b + 1) * BLOCK] = one.T

    key_at = lax.broadcasted_iota(jnp.int32, (TILE, TILE), 0)
    query_at = lax.broadcasted_iota(jnp.int32, (TILE, TILE), 1)

    def self_rows(i):
        mine = slice(i * TILE, (i + 1) * TILE)
        query, grad = tokens_of(0, i), tokens_of(3, i)
        query_docs = jnp.concatenate([doc_row(2 * i), doc_row(2 * i + 1)], axis=1)
        first = max(0, i - 2)
        totals = jnp.zeros((1, TILE), F32)
        deltas = jnp.zeros((1, TILE), F32)
        raws, dnormeds = [], []
        for j in range(first, i + 1):
            there = slice(j * TILE, (j + 1) * TILE)
            key_docs = doc_cols[there]
            visible = jnp.concatenate([key_docs, key_docs], axis=1) == query_docs
            if j == i:
                visible = visible & (key_at <= query_at)
            raw = jnp.where(visible, jnp.exp(dot_nt(tokens_of(1, j), query) * SCALE), 0.0)
            dnormed = dot_nt(tokens_of(2, j), grad)
            totals = totals + jnp.sum(raw, axis=0, keepdims=True)
            deltas = deltas + jnp.sum(raw.astype(BF16).astype(F32) * dnormed, axis=0, keepdims=True)
            raws.append(raw)
            dnormeds.append(dnormed)
        inverse = 1.0 / totals
        deltas = deltas * inverse
        query_sum = jnp.zeros((DH, TILE), F32)
        for j in range(first, i + 1):
            there = slice(j * TILE, (j + 1) * TILE)
            normed = raws[j - first] * inverse
            dscores = (normed * (dnormeds[j - first] - deltas)).astype(BF16)
            query_sum = query_sum + dot(tokens_of(1, j).astype(F32).T.astype(BF16), dscores)
            key_term = dot(dscores, query)
            value_term = dot(normed.astype(BF16), grad)
            if j == i:
                key_acc[there] = key_term
                value_acc[there] = value_term
            else:
                key_acc[there] += key_term
                value_acc[there] += value_term
        grads[0, mine] = (query_sum * SCALE).T.astype(BF16)

    def self_finish():
        grads[1] = (key_acc[...] * SCALE).astype(BF16)
        grads[2] = value_acc[...].astype(BF16)

    def self_back():
        copies = []
        for d in ORDER_BACK:
            there = pl.ds(pl.multiple_of(ctx_peer(d) * BLOCK, 128), BLOCK)
            copies.append(send(
                grads.at[:, there], oself.at[:, :, head_columns(c)],
                s_back.at[d - 1], r_back.at[d - 1], (ctx_peer(d), h, r),
            ))
        here = pl.ds(pl.multiple_of(c * BLOCK, 128), BLOCK)
        return copies, [keep(grads.at[:, here], oself.at[:, :, head_columns(c)])]

    for copy in cross_own:
        copy.wait()

    def pieces(width):
        return [slice(n * width, (n + 1) * width) for n in range(keys_b.shape[2] // width)]

    def project(t):
        here = slice(t * CHUNK, (t + 1) * CHUNK)
        for copy in row_copies[t]:
            copy.wait_recv()
        tokens = rows[:, here, :].reshape(ENTRIES * CHUNK, E)
        for cols in pieces(TILE):
            keys_raw = dot(tokens, wk_v[:, cols])
            values_b[:, here, cols] = dot(tokens, wv_v[:, cols]).astype(BF16).reshape(ENTRIES, CHUNK, TILE)
            for a in range(2):
                one = keys_raw[:, a * DH:(a + 1) * DH]
                mean = jnp.sum(one * one, axis=1, keepdims=True) * (1.0 / DH)
                factor = jnp.broadcast_to(lax.rsqrt(mean + EPSILON), one.shape)
                normed = one * factor
                at = slice(cols.start + a * DH, cols.start + (a + 1) * DH)
                factors[:, here, at] = factor.reshape(ENTRIES, CHUNK, DH)
                keys_n[:, here, at] = normed.reshape(ENTRIES, CHUNK, DH)
                keys_b[:, here, at] = normed.astype(BF16).reshape(ENTRIES, CHUNK, DH)

    for t in range(CHUNKS):
        project(t)

    lanes = lax.broadcasted_iota(jnp.int32, (SPAN, TILE), 1)

    def paired(block):
        low = jnp.where(lanes < DH, block, jnp.zeros_like(block))
        high = jnp.where(lanes >= DH, block, jnp.zeros_like(block))
        return jnp.concatenate([low, high], axis=0)

    def attend(s):
        here = slice(s * SPAN, (s + 1) * SPAN)
        mine = slice(s * NBR, (s + 1) * NBR)
        pairs = pieces(TILE)

        def span_of(array, cols):
            return array[mine, :, cols].reshape(NBR * NR, cols.stop - cols.start)

        queries = [paired(cq_v[here, cols]) for cols in pairs]
        outer = [paired(cg_v[here, cols]) for cols in pairs]
        raws = [jnp.exp(dot_nt(span_of(keys_b, cols), q) * SCALE) for cols, q in zip(pairs, queries)]
        dprobs = [dot_nt(span_of(values_b, cols), g) for cols, g in zip(pairs, outer)]
        probs = [raw * (1.0 / jnp.sum(raw, axis=0, keepdims=True)) for raw in raws]
        probs_b = [p.astype(BF16) for p in probs]
        cdeltas = [jnp.sum(p.astype(F32) * d, axis=0, keepdims=True) for p, d in zip(probs_b, dprobs)]
        dscores = [p * (d - c) for p, d, c in zip(probs, dprobs, cdeltas)]
        dscores_b = [d.astype(BF16) for d in dscores]
        grad_keys = [dot(d, q) * SCALE for d, q in zip(dscores_b, queries)]
        for cols, p, g in zip(pairs, probs_b, outer):
            value_grads[mine, :, cols] = dot(p, g).astype(BF16).reshape(NBR, NR, TILE)
        for cols, d in zip(pairs, dscores):
            part = dot(d.T.astype(BF16), span_of(keys_b, cols)) * SCALE
            cross_out[here, cols.start:cols.start + DH] = part[:SPAN, :DH].astype(BF16)
            cross_out[here, cols.start + DH:cols.stop] = part[SPAN:, DH:].astype(BF16)
        for cols, grad in zip(pairs, grad_keys):
            for a in range(2):
                at = slice(cols.start + a * DH, cols.start + (a + 1) * DH)
                one = grad[:, a * DH:(a + 1) * DH]
                normed = span_of(keys_n, at)
                mean = jnp.sum(normed * one, axis=1, keepdims=True) * (1.0 / DH)
                raw = span_of(factors, at) * (one - normed * mean)
                raw_grads[mine, :, at] = raw.astype(BF16).reshape(NBR, NR, DH)

    for s in range(2):
        attend(s)
    cross_done = keep(cross_out, ocq.at[0])

    def scatter(t):
        here = pl.ds(t * CHUNK, CHUNK)
        shape = (ENTRIES * CHUNK, keys_b.shape[2])
        term = dot_nt(raw_grads[:, here, :].reshape(shape), wk_v[...])
        term = term + dot_nt(value_grads[:, here, :].reshape(shape), wv_v[...])
        for q in range(N_HEAD):
            one = term[:, q * QUARTER:(q + 1) * QUARTER].astype(BF16)
            parts_out[q, :, here, :] = one.reshape(ENTRIES, CHUNK, QUARTER)
        return [
            send(
                parts_out.at[over_head(d), :, here], parts_in.at[h, :, here],
                s_part.at[t * 3 + d - 1], r_part.at[t * 3 + d - 1], (c, over_head(d), r),
            )
            for d in (1, 3, 2)
        ]

    part_copies = [scatter(t) for t in range(CHUNKS)]

    def share(t):
        here = pl.ds(t * CHUNK, CHUNK)
        for copy in part_copies[t]:
            copy.wait_recv()
        total = parts_out[h, :, here, :].astype(F32)
        for d in range(1, N_HEAD):
            total = total + parts_in[over_head(d), :, here, :].astype(F32)
        mine = pl.ds(r * ENTRIES, ENTRIES)
        shares[mine, here] = total.astype(BF16)
        return [
            send(
                shares.at[mine, here], shares.at[mine, here],
                s_share.at[t * 3 + d - 1], r_share.at[t * 3 + d - 1], (c, h, over_ret(d)),
            )
            for d in (1, 3, 2)
        ]

    own_copies = []
    own_kept = []

    def hand_back(t):
        for copy in share_copies[t]:
            copy.wait_recv()
        for k in range(CHUNK // GROUP):
            at = slice(t * CHUNK + k * GROUP, t * CHUNK + (k + 1) * GROUP)
            stacked = shares[:, at].reshape(N_RET * ENTRIES * GROUP, QUARTER)
            summed = dot(selector[...], stacked)
            owned[:, at] = summed.astype(BF16).reshape(N_HEAD * POOL_DEV, GROUP, QUARTER)
        here = pl.ds(t * CHUNK, CHUNK)
        for d in (1, 3, 2):
            own_copies.append(send(
                owned.at[pl.ds(over_head(d) * POOL_DEV, POOL_DEV), here], oenc.at[:, here, my_columns],
                s_own.at[t * 3 + d - 1], r_own.at[t * 3 + d - 1], (c, over_head(d), r),
            ))
        own_kept.append(keep(owned.at[pl.ds(h * POOL_DEV, POOL_DEV), here], oenc.at[:, here, my_columns]))

    back_copies, back_own = [], []
    share_copies = []
    flush(3 * CHUNKS)
    prepare_self()
    self_rows(0)
    self_rows(1)
    share_copies.append(share(0))
    share_copies.append(share(1))
    self_rows(2)
    share_copies.append(share(2))
    share_copies.append(share(3))
    hand_back(0)
    flush(3 + 3 * CHUNKS)
    self_rows(3)
    self_finish()
    hand_back(1)
    back_copies, back_own = self_back()
    hand_back(2)
    hand_back(3)

    cross_done.wait()
    for copy in back_own + own_kept:
        copy.wait()
    for copy in back_copies + own_copies:
        copy.wait_recv()
    flush(0)


def place_outputs(own, cross, pool, *refs):
    targets, sem = refs[:5], refs[5]
    copies = [pltpu.make_async_copy(own.at[a], targets[a].at[0], sem.at[a]) for a in range(3)]
    copies.append(pltpu.make_async_copy(cross, targets[3], sem.at[3]))
    for b in range(POOL_DEV):
        copies.append(pltpu.make_async_copy(pool.at[b], targets[4].at[b], sem.at[4 + b]))
    for copy in copies:
        copy.start()
    for copy in copies:
        copy.wait()


def on_device(
    self_query, self_key, self_value, self_grad, self_docs, cross_query, cross_grad,
    neighbours, encodings, key_weight, value_weight,
):
    block = jax.ShapeDtypeStruct(self_query.shape, BF16)
    any_space = pl.BlockSpec(memory_space=pl.ANY)
    in_specs = [pl.BlockSpec(memory_space=pltpu.HBM)] * 11
    dma = pltpu.SemaphoreType.DMA
    wide = (ENTRIES, NR, key_weight.shape[1])
    scratch = [
        pltpu.SMEM(neighbours.shape, jnp.int32),
        pltpu.VMEM((N_RET, 8, 128), jnp.int32),
        pltpu.SMEM((N_RET, 8, 128), jnp.int32),
        pltpu.VMEM((1, BLOCK), jnp.int32),
        pltpu.VMEM((N_CTX * BLOCK, 128), F32),
        pltpu.VMEM((4 * BLOCK + DOC_ROWS, N_CTX * DH), BF16),
        (pltpu.VMEM((N_HEAD * POOL_DEV, CHUNK, QUARTER), BF16),) * CHUNKS,
        pltpu.VMEM((N_RET * ENTRIES, NR, QUARTER), BF16),
        (pltpu.VMEM((N_RET * ENTRIES, CHUNK, QUARTER), BF16),) * CHUNKS,
        pltpu.VMEM((ENTRIES, NR, E), BF16),
        pltpu.VMEM((N_CTX, 4 * BLOCK + DOC_ROWS, DH), BF16),
        pltpu.VMEM((N_CTX * BLOCK, DH), F32),
        pltpu.VMEM((N_CTX * BLOCK, DH), F32),
        pltpu.VMEM((3, N_CTX * BLOCK, DH), BF16),
        pltpu.VMEM(key_weight.shape, BF16),
        pltpu.VMEM(value_weight.shape, BF16),
        pltpu.VMEM(cross_query.shape[1:], BF16),
        pltpu.VMEM(cross_grad.shape[1:], BF16),
        pltpu.VMEM(cross_grad.shape[1:], BF16),
        pltpu.VMEM(wide, F32),
        pltpu.VMEM(wide, F32),
        pltpu.VMEM(wide, BF16),
        pltpu.VMEM(wide, BF16),
        pltpu.VMEM(wide, BF16),
        pltpu.VMEM(wide, BF16),
        pltpu.VMEM((N_HEAD, ENTRIES, NR, QUARTER), BF16),
        pltpu.VMEM((N_HEAD, ENTRIES, NR, QUARTER), BF16),
        pltpu.VMEM((N_RET * ENTRIES, NR, QUARTER), BF16),
        pltpu.VMEM((N_HEAD * POOL_DEV, NR, QUARTER), BF16),
        pltpu.VMEM((N_HEAD * POOL_DEV * 16, N_RET * ENTRIES * 16), BF16),
        dma((32,)),
        dma((3,)), dma((3,)),
        dma((3 * CHUNKS,)), dma((3 * CHUNKS,)),
        dma((3 * CHUNKS,)), dma((3 * CHUNKS,)),
        dma((3 * CHUNKS,)), dma((3 * CHUNKS,)),
        dma((7,)), dma((7,)),
        dma((3 * CHUNKS,)), dma((3 * CHUNKS,)),
        dma((3 * CHUNKS,)), dma((3 * CHUNKS,)),
        dma((3 * CHUNKS,)), dma((3 * CHUNKS,)),
        dma((7,)), dma((7,)),
    ]
    outs = pl.pallas_call(
        kernel,
        out_shape=(
            jax.ShapeDtypeStruct((3,) + self_query.shape[1:], BF16), block,
            jax.ShapeDtypeStruct(encodings.shape, BF16),
        ),
        in_specs=in_specs,
        out_specs=(any_space,) * 3,
        scratch_shapes=scratch,
        compiler_params=pltpu.CompilerParams(
            collective_id=0, has_side_effects=True, vmem_limit_bytes=32 * 2**20
        ),
        name="retro_backward",
    )(*[
        pltpu.with_memory_space_constraint(array, pltpu.HBM)
        for array in (self_query, self_key, self_value, self_grad, self_docs, cross_query, cross_grad)
    ], pltpu.with_memory_space_constraint(neighbours, pltpu.HBM), *[
        pltpu.with_memory_space_constraint(array, pltpu.HBM)
        for array in (encodings, key_weight, value_weight)
    ])
    return pl.pallas_call(
        place_outputs,
        out_shape=(block, block, block, block, jax.ShapeDtypeStruct(encodings.shape, BF16)),
        in_specs=[any_space] * 3,
        out_specs=(pl.BlockSpec(memory_space=pltpu.HBM),) * 5,
        scratch_shapes=[dma((4 + POOL_DEV,))],
        name="place_outputs",
    )(*[pltpu.with_memory_space_constraint(out, pltpu.VMEM) for out in outs])


def solution(mesh):
    tokens = P("ret", "ctx", "head")
    pool = P(("ctx", "head", "ret"), None, None)
    placed = (
        tokens, tokens, tokens, tokens, P("ret", "ctx"), tokens, tokens,
        P("ret", "ctx", None), pool, P(None, "head"), P(None, "head"),
    )
    return jax.shard_map(
        on_device,
        mesh=mesh,
        in_specs=placed,
        out_specs=(tokens, tokens, tokens, tokens, pool),
        check_vma=False,
    )
```

```python
import functools
import math

import jax
import jax.numpy as jnp
from jax import lax
from jax.experimental import pallas as pl
from jax.experimental.pallas import tpu as pltpu
from jax.sharding import PartitionSpec as P

SPAN = 64
NBR = 2
NR = 128
E = 512
DH = 128
POOL_DEV = 8
EPSILON = 1e-06
SCALE = 1.0 / math.sqrt(DH)

N_CTX = 8
N_HEAD = 4
N_RET = 4
ENTRIES = 4
BLOCK = 128
TILE = 256
DOC_ROWS = 16
QUARTER = E // N_HEAD
FETCH = ((0, 64), (64, 32), (96, 32))
BACK = ((0, 32), (32, 32), (64, 64))
ORDER_BACK = (4, 5, 7, 6, 1, 3, 2)
CHUNKS = len(FETCH)

MESH = pl.DeviceIdType.MESH
F32 = jnp.float32
BF16 = jnp.bfloat16


def dot(a, b):
    return lax.dot_general(a, b, (((1,), (0,)), ((), ())), preferred_element_type=F32)


def dot_nt(a, b):
    return lax.dot_general(a, b, (((1,), (1,)), ((), ())), preferred_element_type=F32)


def kernel(
    sq, sk, sv, sg, docs, cq, cg, nbr, enc, wk, wv,
    oself, ocq, oenc,
    nbr_s, lists_v, lists_s, docs_v, doc_cols, staged, pool, outgoing, incoming, rows, held, key_acc, value_acc, grads,
    wk_v, wv_v, cq_v, cg_v, cross_out, keys_n, factors, keys_b, values_b, raw_grads, value_grads, parts_out, parts_in, shares, owned, selector,
    loc, s_list, r_list, s_pool, r_pool, s_ret, r_ret, s_rows, r_rows, s_self, r_self,
    s_part, r_part, s_share, r_share, s_own, r_own, s_back, r_back,
):
    c, h, r = lax.axis_index("ctx"), lax.axis_index("head"), lax.axis_index("ret")

    def over_ctx(d):
        return lax.rem(c + d, N_CTX)

    def ctx_peer(d):
        far, step = divmod(d, 4)
        half = lax.rem(lax.div(c, 4) + far, 2)
        return half * 4 + lax.rem(lax.rem(c, 4) + step, 4)

    def over_head(d):
        return lax.rem(h + d, N_HEAD)

    def over_ret(d):
        return lax.rem(r + d, N_RET)

    def send(src, dst, ssem, rsem, device):
        copy = pltpu.make_async_remote_copy(
            src_ref=src, dst_ref=dst, send_sem=ssem, recv_sem=rsem,
            device_id=device, device_id_type=MESH,
        )
        copy.start()
        every.append(copy)
        return copy

    every = []

    def flush(left):
        while len(every) > left:
            every.pop(0).wait_send()

    local_count = [0]

    def keep(src, dst):
        copy = pltpu.make_async_copy(src, dst, loc.at[local_count[0]])
        local_count[0] += 1
        copy.start()
        return copy

    wanted_copy = keep(nbr, nbr_s)
    doc_copy = keep(docs, docs_v)
    staging = [
        keep(array.at[0], staged.at[pl.ds(a * BLOCK, BLOCK)]) for a, array in enumerate((sq, sk, sv, sg))
    ]
    barrier = pltpu.get_barrier_semaphore()
    peers = [(over_ctx(d), h, r) for d in range(1, N_CTX)]
    peers += [(c, over_head(d), r) for d in range(1, N_HEAD)]
    peers += [(c, h, over_ret(d)) for d in range(1, N_RET)]
    for peer in peers:
        pl.semaphore_signal(barrier, inc=1, device_id=peer, device_id_type=MESH)
    wanted_copy.wait()
    lane = lax.broadcasted_iota(jnp.int32, (8, 128), 1)
    tile = jnp.zeros((8, 128), jnp.int32)
    for e in range(ENTRIES):
        tile = jnp.where(lane == e, nbr_s[0, e // NBR, e % NBR], tile)
    lists_v[r] = tile
    doc_copy.wait()
    doc_rows = jnp.broadcast_to(docs_v[...].astype(F32), (DOC_ROWS, BLOCK)).astype(BF16)
    for k in range(N_CTX):
        staged[4 * BLOCK:, k * DH:(k + 1) * DH] = doc_rows
    pl.semaphore_wait(barrier, len(peers))

    def quarter_of(owner_column, t):
        return enc.at[:, pl.ds(*FETCH[t]), pl.ds(pl.multiple_of(owner_column * QUARTER, 128), QUARTER)]

    pool_copies = []
    pool_own = []
    for t in range(CHUNKS):
        pool_copies.append([
            send(
                quarter_of(over_head(d), t),
                pool[t].at[pl.ds(h * POOL_DEV, POOL_DEV)],
                s_pool.at[t * 3 + d - 1], r_pool.at[t * 3 + d - 1], (c, over_head(d), r),
            )
            for d in (1, 3, 2)
        ])
        if t == 0:
            list_copies = [
                send(lists_v.at[r], lists_v.at[r], s_list.at[d - 1], r_list.at[d - 1], (c, h, over_ret(d)))
                for d in range(1, N_RET)
            ]
    for t in range(CHUNKS):
        pool_own.append(
            keep(quarter_of(h, t), pool[t].at[pl.ds(h * POOL_DEV, POOL_DEV)])
        )
    self_copies = []
    self_own = []

    def head_columns(number):
        return pl.ds(pl.multiple_of(number * DH, 128), DH)

    def self_start(order):
        for d in order:
            self_copies.append(send(
                staged.at[:, head_columns(ctx_peer(d))], held.at[c],
                s_self.at[d - 1], r_self.at[d - 1], (ctx_peer(d), h, r),
            ))

    for copy in staging:
        copy.wait()
    self_start((4, 6, 1, 3, 2))
    self_own.append(keep(staged.at[:, head_columns(c)], held.at[c]))
    cross_own = [keep(wk, wk_v), keep(wv, wv_v), keep(cq.at[0], cq_v), keep(cg.at[0], cg_v)]

    for copy in list_copies:
        copy.wait_recv()
    to_scalars = keep(lists_v, lists_s)
    to_scalars.wait()

    entries = [[lists_s[q, 0, e] for e in range(ENTRIES)] for q in range(N_RET)]
    places = [[(v >> 5) * POOL_DEV + (v & 7) for v in one] for one in entries]
    wanted_columns = [(lists_s[r, 0, e] >> 3) & 3 for e in range(ENTRIES)]
    ret_copies = []
    row_copies = []
    my_columns = pl.ds(pl.multiple_of(h * QUARTER, 128), QUARTER)

    def hand_out(t):
        here = pl.ds(*FETCH[t])
        pool_own[t].wait()
        for copy in pool_copies[t]:
            copy.wait_recv()
        for q in range(N_RET):
            for e in range(ENTRIES):
                outgoing[q * ENTRIES + e, here] = pool[t][places[q][e]]
        ret_copies.append([
            send(
                outgoing.at[pl.ds(over_ret(d) * ENTRIES, ENTRIES), here],
                incoming[t].at[pl.ds(r * ENTRIES, ENTRIES)],
                s_ret.at[t * 3 + d - 1], r_ret.at[t * 3 + d - 1], (c, h, over_ret(d)),
            )
            for d in (1, 3, 2)
        ])
        incoming[t][pl.ds(r * ENTRIES, ENTRIES)] = outgoing[pl.ds(r * ENTRIES, ENTRIES), here]

    def spread(t):
        here = pl.ds(*FETCH[t])
        for copy in ret_copies[t]:
            copy.wait_recv()
        for e in range(ENTRIES):
            rows[e, here, my_columns] = incoming[t][wanted_columns[e] * ENTRIES + e]
        row_copies.append([
            send(
                rows.at[:, here, my_columns], rows.at[:, here, my_columns],
                s_rows.at[t * 3 + d - 1], r_rows.at[t * 3 + d - 1], (c, over_head(d), r),
            )
            for d in (1, 3, 2)
        ])

    for t in range(CHUNKS + 1):
        if t < CHUNKS:
            hand_out(t)
        if t == CHUNKS - 1:
            self_start((5, 7))
        if t >= 1:
            spread(t - 1)

    GROUP = 16
    lane_e = lax.broadcasted_iota(jnp.int32, (1, N_RET * ENTRIES * GROUP), 1)
    named = jnp.zeros((1, N_RET * ENTRIES * GROUP), jnp.int32)
    for q in range(N_RET):
        for e in range(ENTRIES):
            k = q * ENTRIES + e
            named = jnp.where(lane_e // GROUP == k, entries[q][e], named)
    wide = (N_HEAD * POOL_DEV * GROUP, N_RET * ENTRIES * GROUP)
    target = lax.broadcasted_iota(jnp.int32, wide, 0)
    slot = target // GROUP
    wanted = ((slot // POOL_DEV) * N_RET + r) * POOL_DEV + slot % POOL_DEV
    same_token = target % GROUP == lax.broadcasted_iota(jnp.int32, wide, 1) % GROUP
    selector[...] = jnp.where((wanted == named) & same_token, 1.0, 0.0).astype(BF16)

    def doc_row(b):
        return held[b, 4 * BLOCK:, :].astype(F32)[:1]

    def tokens_of(a, i):
        return held[2 * i:2 * i + 2, a * BLOCK:(a + 1) * BLOCK, :].reshape(TILE, DH)

    def prepare_self():
        for copy in self_copies:
            copy.wait_recv()
        for copy in self_own:
            copy.wait()
        for b in range(N_CTX):
            one = jnp.broadcast_to(doc_row(b), (BLOCK, BLOCK))
            doc_cols[b * BLOCK:(b + 1) * BLOCK] = one.T

    key_at = lax.broadcasted_iota(jnp.int32, (TILE, TILE), 0)
    query_at = lax.broadcasted_iota(jnp.int32, (TILE, TILE), 1)

    def self_rows(i):
        mine = slice(i * TILE, (i + 1) * TILE)
        query, grad = tokens_of(0, i), tokens_of(3, i)
        query_docs = jnp.concatenate([doc_row(2 * i), doc_row(2 * i + 1)], axis=1)
        first = max(0, i - 2)
        totals = jnp.zeros((1, TILE), F32)
        deltas = jnp.zeros((1, TILE), F32)
        raws, dnormeds = [], []
        for j in range(first, i + 1):
            there = slice(j * TILE, (j + 1) * TILE)
            key_docs = doc_cols[there]
            visible = jnp.concatenate([key_docs, key_docs], axis=1) == query_docs
            if j == i:
                visible = visible & (key_at <= query_at)
            raw = jnp.where(visible, jnp.exp(dot_nt(tokens_of(1, j), query) * SCALE), 0.0)
            dnormed = dot_nt(tokens_of(2, j), grad)
            totals = totals + jnp.sum(raw, axis=0, keepdims=True)
            deltas = deltas + jnp.sum(raw.astype(BF16).astype(F32) * dnormed, axis=0, keepdims=True)
            raws.append(raw)
            dnormeds.append(dnormed)
        inverse = 1.0 / totals
        deltas = deltas * inverse
        query_sum = jnp.zeros((DH, TILE), F32)
        for j in range(first, i + 1):
            there = slice(j * TILE, (j + 1) * TILE)
            normed = raws[j - first] * inverse
            dscores = (normed * (dnormeds[j - first] - deltas)).astype(BF16)
            query_sum = query_sum + dot(tokens_of(1, j).astype(F32).T.astype(BF16), dscores)
            key_term = dot(dscores, query)
            value_term = dot(normed.astype(BF16), grad)
            if j == i:
                key_acc[there] = key_term
                value_acc[there] = value_term
            else:
                key_acc[there] += key_term
                value_acc[there] += value_term
        grads[0, mine] = (query_sum * SCALE).T.astype(BF16)

    def self_finish():
        grads[1] = (key_acc[...] * SCALE).astype(BF16)
        grads[2] = value_acc[...].astype(BF16)

    def self_back():
        copies = []
        for d in ORDER_BACK:
            there = pl.ds(pl.multiple_of(ctx_peer(d) * BLOCK, 128), BLOCK)
            copies.append(send(
                grads.at[:, there], oself.at[:, :, head_columns(c)],
                s_back.at[d - 1], r_back.at[d - 1], (ctx_peer(d), h, r),
            ))
        here = pl.ds(pl.multiple_of(c * BLOCK, 128), BLOCK)
        return copies, [keep(grads.at[:, here], oself.at[:, :, head_columns(c)])]

    for copy in cross_own:
        copy.wait()

    def pieces(width):
        return [slice(n * width, (n + 1) * width) for n in range(keys_b.shape[2] // width)]

    def project(t):
        first, size = FETCH[t]
        here = slice(first, first + size)
        for copy in row_copies[t]:
            copy.wait_recv()
        tokens = rows[:, here, :].reshape(ENTRIES * size, E)
        for cols in pieces(TILE):
            keys_raw = dot(tokens, wk_v[:, cols])
            values_b[:, here, cols] = dot(tokens, wv_v[:, cols]).astype(BF16).reshape(ENTRIES, size, TILE)
            for a in range(2):
                one = keys_raw[:, a * DH:(a + 1) * DH]
                mean = jnp.sum(one * one, axis=1, keepdims=True) * (1.0 / DH)
                factor = jnp.broadcast_to(lax.rsqrt(mean + EPSILON), one.shape)
                normed = one * factor
                at = slice(cols.start + a * DH, cols.start + (a + 1) * DH)
                factors[:, here, at] = factor.reshape(ENTRIES, size, DH)
                keys_n[:, here, at] = normed.reshape(ENTRIES, size, DH)
                keys_b[:, here, at] = normed.astype(BF16).reshape(ENTRIES, size, DH)

    for t in range(CHUNKS):
        project(t)

    lanes = lax.broadcasted_iota(jnp.int32, (SPAN, TILE), 1)

    def paired(block):
        low = jnp.where(lanes < DH, block, jnp.zeros_like(block))
        high = jnp.where(lanes >= DH, block, jnp.zeros_like(block))
        return jnp.concatenate([low, high], axis=0)

    def attend(s):
        here = slice(s * SPAN, (s + 1) * SPAN)
        mine = slice(s * NBR, (s + 1) * NBR)
        pairs = pieces(TILE)

        def span_of(array, cols):
            return array[mine, :, cols].reshape(NBR * NR, cols.stop - cols.start)

        queries = [paired(cq_v[here, cols]) for cols in pairs]
        outer = [paired(cg_v[here, cols]) for cols in pairs]
        raws = [jnp.exp(dot_nt(span_of(keys_b, cols), q) * SCALE) for cols, q in zip(pairs, queries)]
        dprobs = [dot_nt(span_of(values_b, cols), g) for cols, g in zip(pairs, outer)]
        probs = [raw * (1.0 / jnp.sum(raw, axis=0, keepdims=True)) for raw in raws]
        probs_b = [p.astype(BF16) for p in probs]
        cdeltas = [jnp.sum(p.astype(F32) * d, axis=0, keepdims=True) for p, d in zip(probs_b, dprobs)]
        dscores = [p * (d - c) for p, d, c in zip(probs, dprobs, cdeltas)]
        dscores_b = [d.astype(BF16) for d in dscores]
        grad_keys = [dot(d, q) * SCALE for d, q in zip(dscores_b, queries)]
        for cols, p, g in zip(pairs, probs_b, outer):
            value_grads[mine, :, cols] = dot(p, g).astype(BF16).reshape(NBR, NR, TILE)
        for cols, d in zip(pairs, dscores):
            part = dot(d.T.astype(BF16), span_of(keys_b, cols)) * SCALE
            cross_out[here, cols.start:cols.start + DH] = part[:SPAN, :DH].astype(BF16)
            cross_out[here, cols.start + DH:cols.stop] = part[SPAN:, DH:].astype(BF16)
        for cols, grad in zip(pairs, grad_keys):
            for a in range(2):
                at = slice(cols.start + a * DH, cols.start + (a + 1) * DH)
                one = grad[:, a * DH:(a + 1) * DH]
                normed = span_of(keys_n, at)
                mean = jnp.sum(normed * one, axis=1, keepdims=True) * (1.0 / DH)
                raw = span_of(factors, at) * (one - normed * mean)
                raw_grads[mine, :, at] = raw.astype(BF16).reshape(NBR, NR, DH)

    for s in range(2):
        attend(s)
    cross_done = keep(cross_out, ocq.at[0])

    def scatter(t):
        first, size = BACK[t]
        here = pl.ds(first, size)
        shape = (ENTRIES * size, keys_b.shape[2])
        term = dot_nt(raw_grads[:, here, :].reshape(shape), wk_v[...])
        term = term + dot_nt(value_grads[:, here, :].reshape(shape), wv_v[...])
        for q in range(N_HEAD):
            one = term[:, q * QUARTER:(q + 1) * QUARTER].astype(BF16)
            parts_out[q, :, here, :] = one.reshape(ENTRIES, size, QUARTER)
        return [
            send(
                parts_out.at[over_head(d), :, here], parts_in.at[h, :, here],
                s_part.at[t * 3 + d - 1], r_part.at[t * 3 + d - 1], (c, over_head(d), r),
            )
            for d in (1, 3, 2)
        ]

    part_copies = [scatter(t) for t in range(CHUNKS)]

    def share(t):
        first, size = BACK[t]
        here = pl.ds(first, size)
        for copy in part_copies[t]:
            copy.wait_recv()
        total = parts_out[h, :, here, :].astype(F32)
        for d in range(1, N_HEAD):
            total = total + parts_in[over_head(d), :, here, :].astype(F32)
        mine = pl.ds(r * ENTRIES, ENTRIES)
        shares[mine, here] = total.astype(BF16)
        return [
            send(
                shares.at[mine, here], shares.at[mine, here],
                s_share.at[t * 3 + d - 1], r_share.at[t * 3 + d - 1], (c, h, over_ret(d)),
            )
            for d in (1, 3, 2)
        ]

    own_copies = []
    own_kept = []

    def hand_back(t):
        for copy in share_copies[t]:
            copy.wait_recv()
        first, size = BACK[t]
        for k in range(size // GROUP):
            at = slice(first + k * GROUP, first + (k + 1) * GROUP)
            stacked = shares[:, at].reshape(N_RET * ENTRIES * GROUP, QUARTER)
            summed = dot(selector[...], stacked)
            owned[:, at] = summed.astype(BF16).reshape(N_HEAD * POOL_DEV, GROUP, QUARTER)
        first, size = BACK[t]
        here = pl.ds(first, size)
        for d in (1, 3, 2):
            own_copies.append(send(
                owned.at[pl.ds(over_head(d) * POOL_DEV, POOL_DEV), here], oenc.at[:, here, my_columns],
                s_own.at[t * 3 + d - 1], r_own.at[t * 3 + d - 1], (c, over_head(d), r),
            ))
        own_kept.append(keep(owned.at[pl.ds(h * POOL_DEV, POOL_DEV), here], oenc.at[:, here, my_columns]))

    back_copies, back_own = [], []
    share_copies = []
    flush(3 * CHUNKS)
    prepare_self()
    self_rows(0)
    self_rows(1)
    share_copies.append(share(0))
    self_rows(2)
    share_copies.append(share(1))
    self_rows(3)
    self_finish()
    share_copies.append(share(2))
    back_copies, back_own = self_back()
    hand_back(0)
    hand_back(1)
    hand_back(2)

    cross_done.wait()
    for copy in back_own + own_kept:
        copy.wait()
    for copy in back_copies + own_copies:
        copy.wait_recv()
    flush(0)


def place_outputs(own, cross, pool, *refs):
    targets, sem = refs[:5], refs[5]
    copies = [pltpu.make_async_copy(own.at[a], targets[a].at[0], sem.at[a]) for a in range(3)]
    copies.append(pltpu.make_async_copy(cross, targets[3], sem.at[3]))
    for b in range(POOL_DEV):
        copies.append(pltpu.make_async_copy(pool.at[b], targets[4].at[b], sem.at[4 + b]))
    for copy in copies:
        copy.start()
    for copy in copies:
        copy.wait()


def on_device(
    self_query, self_key, self_value, self_grad, self_docs, cross_query, cross_grad,
    neighbours, encodings, key_weight, value_weight,
):
    block = jax.ShapeDtypeStruct(self_query.shape, BF16)
    any_space = pl.BlockSpec(memory_space=pl.ANY)
    in_specs = [pl.BlockSpec(memory_space=pltpu.HBM)] * 11
    dma = pltpu.SemaphoreType.DMA
    wide = (ENTRIES, NR, key_weight.shape[1])
    scratch = [
        pltpu.SMEM(neighbours.shape, jnp.int32),
        pltpu.VMEM((N_RET, 8, 128), jnp.int32),
        pltpu.SMEM((N_RET, 8, 128), jnp.int32),
        pltpu.VMEM((1, BLOCK), jnp.int32),
        pltpu.VMEM((N_CTX * BLOCK, 128), F32),
        pltpu.VMEM((4 * BLOCK + DOC_ROWS, N_CTX * DH), BF16),
        tuple(pltpu.VMEM((N_HEAD * POOL_DEV, size, QUARTER), BF16) for _, size in FETCH),
        pltpu.VMEM((N_RET * ENTRIES, NR, QUARTER), BF16),
        tuple(pltpu.VMEM((N_RET * ENTRIES, size, QUARTER), BF16) for _, size in FETCH),
        pltpu.VMEM((ENTRIES, NR, E), BF16),
        pltpu.VMEM((N_CTX, 4 * BLOCK + DOC_ROWS, DH), BF16),
        pltpu.VMEM((N_CTX * BLOCK, DH), F32),
        pltpu.VMEM((N_CTX * BLOCK, DH), F32),
        pltpu.VMEM((3, N_CTX * BLOCK, DH), BF16),
        pltpu.VMEM(key_weight.shape, BF16),
        pltpu.VMEM(value_weight.shape, BF16),
        pltpu.VMEM(cross_query.shape[1:], BF16),
        pltpu.VMEM(cross_grad.shape[1:], BF16),
        pltpu.VMEM(cross_grad.shape[1:], BF16),
        pltpu.VMEM(wide, F32),
        pltpu.VMEM(wide, F32),
        pltpu.VMEM(wide, BF16),
        pltpu.VMEM(wide, BF16),
        pltpu.VMEM(wide, BF16),
        pltpu.VMEM(wide, BF16),
        pltpu.VMEM((N_HEAD, ENTRIES, NR, QUARTER), BF16),
        pltpu.VMEM((N_HEAD, ENTRIES, NR, QUARTER), BF16),
        pltpu.VMEM((N_RET * ENTRIES, NR, QUARTER), BF16),
        pltpu.VMEM((N_HEAD * POOL_DEV, NR, QUARTER), BF16),
        pltpu.VMEM((N_HEAD * POOL_DEV * 16, N_RET * ENTRIES * 16), BF16),
        dma((32,)),
        dma((3,)), dma((3,)),
        dma((3 * CHUNKS,)), dma((3 * CHUNKS,)),
        dma((3 * CHUNKS,)), dma((3 * CHUNKS,)),
        dma((3 * CHUNKS,)), dma((3 * CHUNKS,)),
        dma((7,)), dma((7,)),
        dma((3 * CHUNKS,)), dma((3 * CHUNKS,)),
        dma((3 * CHUNKS,)), dma((3 * CHUNKS,)),
        dma((3 * CHUNKS,)), dma((3 * CHUNKS,)),
        dma((7,)), dma((7,)),
    ]
    outs = pl.pallas_call(
        kernel,
        out_shape=(
            jax.ShapeDtypeStruct((3,) + self_query.shape[1:], BF16), block,
            jax.ShapeDtypeStruct(encodings.shape, BF16),
        ),
        in_specs=in_specs,
        out_specs=(any_space,) * 3,
        scratch_shapes=scratch,
        compiler_params=pltpu.CompilerParams(
            collective_id=0, has_side_effects=True, vmem_limit_bytes=32 * 2**20
        ),
        name="retro_backward",
    )(*[
        pltpu.with_memory_space_constraint(array, pltpu.HBM)
        for array in (self_query, self_key, self_value, self_grad, self_docs, cross_query, cross_grad)
    ], pltpu.with_memory_space_constraint(neighbours, pltpu.HBM), *[
        pltpu.with_memory_space_constraint(array, pltpu.HBM)
        for array in (encodings, key_weight, value_weight)
    ])
    return pl.pallas_call(
        place_outputs,
        out_shape=(block, block, block, block, jax.ShapeDtypeStruct(encodings.shape, BF16)),
        in_specs=[any_space] * 3,
        out_specs=(pl.BlockSpec(memory_space=pltpu.HBM),) * 5,
        scratch_shapes=[dma((4 + POOL_DEV,))],
        name="place_outputs",
    )(*[pltpu.with_memory_space_constraint(out, pltpu.VMEM) for out in outs])


def solution(mesh):
    tokens = P("ret", "ctx", "head")
    pool = P(("ctx", "head", "ret"), None, None)
    placed = (
        tokens, tokens, tokens, tokens, P("ret", "ctx"), tokens, tokens,
        P("ret", "ctx", None), pool, P(None, "head"), P(None, "head"),
    )
    return jax.shard_map(
        on_device,
        mesh=mesh,
        in_specs=placed,
        out_specs=(tokens, tokens, tokens, tokens, pool),
        check_vma=False,
    )
```

```python
import functools
import math

import jax
import jax.numpy as jnp
from jax import lax
from jax.experimental import pallas as pl
from jax.experimental.pallas import tpu as pltpu
from jax.sharding import PartitionSpec as P

SPAN = 64
NBR = 2
NR = 128
E = 512
DH = 128
POOL_DEV = 8
EPSILON = 1e-06
SCALE = 1.0 / math.sqrt(DH)

N_CTX = 8
N_HEAD = 4
N_RET = 4
ENTRIES = 4
BLOCK = 128
TILE = 256
DOC_ROWS = 16
QUARTER = E // N_HEAD
FETCH = ((0, 64), (64, 32), (96, 32))
BACK = ((0, 32), (32, 32), (64, 64))
ORDER_BACK = (6, 5, 7, 4, 2, 1, 3)
CHUNKS = len(FETCH)

MESH = pl.DeviceIdType.MESH
F32 = jnp.float32
BF16 = jnp.bfloat16


def dot(a, b):
    return lax.dot_general(a, b, (((1,), (0,)), ((), ())), preferred_element_type=F32)


def dot_nt(a, b):
    return lax.dot_general(a, b, (((1,), (1,)), ((), ())), preferred_element_type=F32)


def kernel(
    sq, sk, sv, sg, docs, cq, cg, nbr, enc, wk, wv,
    oself, ocq, oenc,
    nbr_s, lists_v, lists_s, docs_v, doc_cols, staged, pool, outgoing, incoming, rows, held, key_acc, value_acc, grads,
    wk_v, wv_v, cq_v, cg_v, cross_out, keys_n, factors, keys_b, values_b, raw_grads, value_grads, parts_out, parts_in, shares, owned, selector,
    loc, s_list, r_list, s_pool, r_pool, s_ret, r_ret, s_rows, r_rows, s_self, r_self,
    s_part, r_part, s_share, r_share, s_own, r_own, s_back, r_back,
):
    c, h, r = lax.axis_index("ctx"), lax.axis_index("head"), lax.axis_index("ret")

    def over_ctx(d):
        return lax.rem(c + d, N_CTX)

    def ctx_peer(d):
        far, step = divmod(d, 4)
        half = lax.rem(lax.div(c, 4) + far, 2)
        return half * 4 + lax.rem(lax.rem(c, 4) + step, 4)

    def over_head(d):
        return lax.rem(h + d, N_HEAD)

    def over_ret(d):
        return lax.rem(r + d, N_RET)

    def send(src, dst, ssem, rsem, device):
        copy = pltpu.make_async_remote_copy(
            src_ref=src, dst_ref=dst, send_sem=ssem, recv_sem=rsem,
            device_id=device, device_id_type=MESH,
        )
        copy.start()
        every.append(copy)
        return copy

    every = []

    def flush(left):
        while len(every) > left:
            every.pop(0).wait_send()

    local_count = [0]

    def keep(src, dst):
        copy = pltpu.make_async_copy(src, dst, loc.at[local_count[0]])
        local_count[0] += 1
        copy.start()
        return copy

    wanted_copy = keep(nbr, nbr_s)
    doc_copy = keep(docs, docs_v)
    staging = [
        keep(array.at[0], staged.at[pl.ds(a * BLOCK, BLOCK)]) for a, array in enumerate((sq, sk, sv, sg))
    ]
    barrier = pltpu.get_barrier_semaphore()
    peers = [(over_ctx(d), h, r) for d in range(1, N_CTX)]
    peers += [(c, over_head(d), r) for d in range(1, N_HEAD)]
    peers += [(c, h, over_ret(d)) for d in range(1, N_RET)]
    for peer in peers:
        pl.semaphore_signal(barrier, inc=1, device_id=peer, device_id_type=MESH)
    wanted_copy.wait()
    lane = lax.broadcasted_iota(jnp.int32, (8, 128), 1)
    tile = jnp.zeros((8, 128), jnp.int32)
    for e in range(ENTRIES):
        tile = jnp.where(lane == e, nbr_s[0, e // NBR, e % NBR], tile)
    lists_v[r] = tile
    doc_copy.wait()
    doc_rows = jnp.broadcast_to(docs_v[...].astype(F32), (DOC_ROWS, BLOCK)).astype(BF16)
    for k in range(N_CTX):
        staged[4 * BLOCK:, k * DH:(k + 1) * DH] = doc_rows
    pl.semaphore_wait(barrier, len(peers))

    def quarter_of(owner_column, t):
        return enc.at[:, pl.ds(*FETCH[t]), pl.ds(pl.multiple_of(owner_column * QUARTER, 128), QUARTER)]

    pool_copies = []
    pool_own = []
    for t in range(CHUNKS):
        pool_copies.append([
            send(
                quarter_of(over_head(d), t),
                pool[t].at[pl.ds(h * POOL_DEV, POOL_DEV)],
                s_pool.at[t * 3 + d - 1], r_pool.at[t * 3 + d - 1], (c, over_head(d), r),
            )
            for d in (1, 3, 2)
        ])
        if t == 0:
            list_copies = [
                send(lists_v.at[r], lists_v.at[r], s_list.at[d - 1], r_list.at[d - 1], (c, h, over_ret(d)))
                for d in range(1, N_RET)
            ]
    for t in range(CHUNKS):
        pool_own.append(
            keep(quarter_of(h, t), pool[t].at[pl.ds(h * POOL_DEV, POOL_DEV)])
        )
    self_copies = []
    self_own = []

    def head_columns(number):
        return pl.ds(pl.multiple_of(number * DH, 128), DH)

    def self_start(order):
        for d in order:
            self_copies.append(send(
                staged.at[:, head_columns(ctx_peer(d))], held.at[c],
                s_self.at[d - 1], r_self.at[d - 1], (ctx_peer(d), h, r),
            ))

    for copy in staging:
        copy.wait()
    self_start((4, 6, 1, 3, 2))
    self_own.append(keep(staged.at[:, head_columns(c)], held.at[c]))
    cross_own = [keep(wk, wk_v), keep(wv, wv_v), keep(cq.at[0], cq_v), keep(cg.at[0], cg_v)]

    for copy in list_copies:
        copy.wait_recv()
    to_scalars = keep(lists_v, lists_s)
    to_scalars.wait()

    entries = [[lists_s[q, 0, e] for e in range(ENTRIES)] for q in range(N_RET)]
    places = [[(v >> 5) * POOL_DEV + (v & 7) for v in one] for one in entries]
    wanted_columns = [(lists_s[r, 0, e] >> 3) & 3 for e in range(ENTRIES)]
    ret_copies = []
    row_copies = []
    my_columns = pl.ds(pl.multiple_of(h * QUARTER, 128), QUARTER)

    def hand_out(t):
        here = pl.ds(*FETCH[t])
        pool_own[t].wait()
        for copy in pool_copies[t]:
            copy.wait_recv()
        for q in range(N_RET):
            for e in range(ENTRIES):
                outgoing[q * ENTRIES + e, here] = pool[t][places[q][e]]
        ret_copies.append([
            send(
                outgoing.at[pl.ds(over_ret(d) * ENTRIES, ENTRIES), here],
                incoming[t].at[pl.ds(r * ENTRIES, ENTRIES)],
                s_ret.at[t * 3 + d - 1], r_ret.at[t * 3 + d - 1], (c, h, over_ret(d)),
            )
            for d in (1, 3, 2)
        ])
        incoming[t][pl.ds(r * ENTRIES, ENTRIES)] = outgoing[pl.ds(r * ENTRIES, ENTRIES), here]

    def spread(t):
        here = pl.ds(*FETCH[t])
        for copy in ret_copies[t]:
            copy.wait_recv()
        for e in range(ENTRIES):
            rows[e, here, my_columns] = incoming[t][wanted_columns[e] * ENTRIES + e]
        row_copies.append([
            send(
                rows.at[:, here, my_columns], rows.at[:, here, my_columns],
                s_rows.at[t * 3 + d - 1], r_rows.at[t * 3 + d - 1], (c, over_head(d), r),
            )
            for d in (1, 3, 2)
        ])

    for t in range(CHUNKS + 1):
        if t < CHUNKS:
            hand_out(t)
        if t == CHUNKS - 1:
            self_start((5, 7))
        if t >= 1:
            spread(t - 1)

    GROUP = 16
    lane_e = lax.broadcasted_iota(jnp.int32, (1, N_RET * ENTRIES * GROUP), 1)
    named = jnp.zeros((1, N_RET * ENTRIES * GROUP), jnp.int32)
    for q in range(N_RET):
        for e in range(ENTRIES):
            k = q * ENTRIES + e
            named = jnp.where(lane_e // GROUP == k, entries[q][e], named)
    wide = (N_HEAD * POOL_DEV * GROUP, N_RET * ENTRIES * GROUP)
    target = lax.broadcasted_iota(jnp.int32, wide, 0)
    slot = target // GROUP
    wanted = ((slot // POOL_DEV) * N_RET + r) * POOL_DEV + slot % POOL_DEV
    same_token = target % GROUP == lax.broadcasted_iota(jnp.int32, wide, 1) % GROUP
    selector[...] = jnp.where((wanted == named) & same_token, 1.0, 0.0).astype(BF16)

    def doc_row(b):
        return held[b, 4 * BLOCK:, :].astype(F32)[:1]

    def tokens_of(a, i):
        return held[2 * i:2 * i + 2, a * BLOCK:(a + 1) * BLOCK, :].reshape(TILE, DH)

    def prepare_self():
        for copy in self_copies:
            copy.wait_recv()
        for copy in self_own:
            copy.wait()
        for b in range(N_CTX):
            one = jnp.broadcast_to(doc_row(b), (BLOCK, BLOCK))
            doc_cols[b * BLOCK:(b + 1) * BLOCK] = one.T

    key_at = lax.broadcasted_iota(jnp.int32, (TILE, TILE), 0)
    query_at = lax.broadcasted_iota(jnp.int32, (TILE, TILE), 1)

    def self_rows(i):
        mine = slice(i * TILE, (i + 1) * TILE)
        query, grad = tokens_of(0, i), tokens_of(3, i)
        query_docs = jnp.concatenate([doc_row(2 * i), doc_row(2 * i + 1)], axis=1)
        first = max(0, i - 2)
        totals = jnp.zeros((1, TILE), F32)
        deltas = jnp.zeros((1, TILE), F32)
        raws, dnormeds = [], []
        for j in range(first, i + 1):
            there = slice(j * TILE, (j + 1) * TILE)
            key_docs = doc_cols[there]
            visible = jnp.concatenate([key_docs, key_docs], axis=1) == query_docs
            if j == i:
                visible = visible & (key_at <= query_at)
            raw = jnp.where(visible, jnp.exp(dot_nt(tokens_of(1, j), query) * SCALE), 0.0)
            dnormed = dot_nt(tokens_of(2, j), grad)
            totals = totals + jnp.sum(raw, axis=0, keepdims=True)
            deltas = deltas + jnp.sum(raw.astype(BF16).astype(F32) * dnormed, axis=0, keepdims=True)
            raws.append(raw)
            dnormeds.append(dnormed)
        inverse = 1.0 / totals
        deltas = deltas * inverse
        query_sum = jnp.zeros((DH, TILE), F32)
        for j in range(first, i + 1):
            there = slice(j * TILE, (j + 1) * TILE)
            normed = raws[j - first] * inverse
            dscores = (normed * (dnormeds[j - first] - deltas)).astype(BF16)
            query_sum = query_sum + dot(tokens_of(1, j).astype(F32).T.astype(BF16), dscores)
            key_term = dot(dscores, query)
            value_term = dot(normed.astype(BF16), grad)
            if j == i:
                key_acc[there] = key_term
                value_acc[there] = value_term
            else:
                key_acc[there] += key_term
                value_acc[there] += value_term
        grads[0, mine] = (query_sum * SCALE).T.astype(BF16)

    def self_finish():
        grads[1] = (key_acc[...] * SCALE).astype(BF16)
        grads[2] = value_acc[...].astype(BF16)

    def self_back():
        copies = []
        for d in ORDER_BACK:
            there = pl.ds(pl.multiple_of(ctx_peer(d) * BLOCK, 128), BLOCK)
            copies.append(send(
                grads.at[:, there], oself.at[:, :, head_columns(c)],
                s_back.at[d - 1], r_back.at[d - 1], (ctx_peer(d), h, r),
            ))
        here = pl.ds(pl.multiple_of(c * BLOCK, 128), BLOCK)
        return copies, [keep(grads.at[:, here], oself.at[:, :, head_columns(c)])]

    for copy in cross_own:
        copy.wait()

    def pieces(width):
        return [slice(n * width, (n + 1) * width) for n in range(keys_b.shape[2] // width)]

    def project(t):
        first, size = FETCH[t]
        here = slice(first, first + size)
        for copy in row_copies[t]:
            copy.wait_recv()
        tokens = rows[:, here, :].reshape(ENTRIES * size, E)
        for cols in pieces(TILE):
            keys_raw = dot(tokens, wk_v[:, cols])
            values_b[:, here, cols] = dot(tokens, wv_v[:, cols]).astype(BF16).reshape(ENTRIES, size, TILE)
            for a in range(2):
                one = keys_raw[:, a * DH:(a + 1) * DH]
                mean = jnp.sum(one * one, axis=1, keepdims=True) * (1.0 / DH)
                factor = jnp.broadcast_to(lax.rsqrt(mean + EPSILON), one.shape)
                normed = one * factor
                at = slice(cols.start + a * DH, cols.start + (a + 1) * DH)
                factors[:, here, at] = factor.reshape(ENTRIES, size, DH)
                keys_n[:, here, at] = normed.reshape(ENTRIES, size, DH)
                keys_b[:, here, at] = normed.astype(BF16).reshape(ENTRIES, size, DH)

    for t in range(CHUNKS):
        project(t)

    lanes = lax.broadcasted_iota(jnp.int32, (SPAN, TILE), 1)

    def paired(block):
        low = jnp.where(lanes < DH, block, jnp.zeros_like(block))
        high = jnp.where(lanes >= DH, block, jnp.zeros_like(block))
        return jnp.concatenate([low, high], axis=0)

    def attend(s):
        here = slice(s * SPAN, (s + 1) * SPAN)
        mine = slice(s * NBR, (s + 1) * NBR)
        pairs = pieces(TILE)

        def span_of(array, cols):
            return array[mine, :, cols].reshape(NBR * NR, cols.stop - cols.start)

        queries = [paired(cq_v[here, cols]) for cols in pairs]
        outer = [paired(cg_v[here, cols]) for cols in pairs]
        raws = [jnp.exp(dot_nt(span_of(keys_b, cols), q) * SCALE) for cols, q in zip(pairs, queries)]
        dprobs = [dot_nt(span_of(values_b, cols), g) for cols, g in zip(pairs, outer)]
        probs = [raw * (1.0 / jnp.sum(raw, axis=0, keepdims=True)) for raw in raws]
        probs_b = [p.astype(BF16) for p in probs]
        cdeltas = [jnp.sum(p.astype(F32) * d, axis=0, keepdims=True) for p, d in zip(probs_b, dprobs)]
        dscores = [p * (d - c) for p, d, c in zip(probs, dprobs, cdeltas)]
        dscores_b = [d.astype(BF16) for d in dscores]
        grad_keys = [dot(d, q) * SCALE for d, q in zip(dscores_b, queries)]
        for cols, p, g in zip(pairs, probs_b, outer):
            value_grads[mine, :, cols] = dot(p, g).astype(BF16).reshape(NBR, NR, TILE)
        for cols, d in zip(pairs, dscores):
            part = dot(d.T.astype(BF16), span_of(keys_b, cols)) * SCALE
            cross_out[here, cols.start:cols.start + DH] = part[:SPAN, :DH].astype(BF16)
            cross_out[here, cols.start + DH:cols.stop] = part[SPAN:, DH:].astype(BF16)
        for cols, grad in zip(pairs, grad_keys):
            for a in range(2):
                at = slice(cols.start + a * DH, cols.start + (a + 1) * DH)
                one = grad[:, a * DH:(a + 1) * DH]
                normed = span_of(keys_n, at)
                mean = jnp.sum(normed * one, axis=1, keepdims=True) * (1.0 / DH)
                raw = span_of(factors, at) * (one - normed * mean)
                raw_grads[mine, :, at] = raw.astype(BF16).reshape(NBR, NR, DH)

    for s in range(2):
        attend(s)
    cross_done = keep(cross_out, ocq.at[0])

    def scatter(t):
        first, size = BACK[t]
        here = pl.ds(first, size)
        shape = (ENTRIES * size, keys_b.shape[2])
        term = dot_nt(raw_grads[:, here, :].reshape(shape), wk_v[...])
        term = term + dot_nt(value_grads[:, here, :].reshape(shape), wv_v[...])
        for q in range(N_HEAD):
            one = term[:, q * QUARTER:(q + 1) * QUARTER].astype(BF16)
            parts_out[q, :, here, :] = one.reshape(ENTRIES, size, QUARTER)
        return [
            send(
                parts_out.at[over_head(d), :, here], parts_in.at[h, :, here],
                s_part.at[t * 3 + d - 1], r_part.at[t * 3 + d - 1], (c, over_head(d), r),
            )
            for d in (1, 3, 2)
        ]

    part_copies = [scatter(t) for t in range(CHUNKS)]

    def share(t):
        first, size = BACK[t]
        here = pl.ds(first, size)
        for copy in part_copies[t]:
            copy.wait_recv()
        total = parts_out[h, :, here, :].astype(F32)
        for d in range(1, N_HEAD):
            total = total + parts_in[over_head(d), :, here, :].astype(F32)
        mine = pl.ds(r * ENTRIES, ENTRIES)
        shares[mine, here] = total.astype(BF16)
        return [
            send(
                shares.at[mine, here], shares.at[mine, here],
                s_share.at[t * 3 + d - 1], r_share.at[t * 3 + d - 1], (c, h, over_ret(d)),
            )
            for d in (1, 3, 2)
        ]

    own_copies = []
    own_kept = []

    def hand_back(t):
        for copy in share_copies[t]:
            copy.wait_recv()
        first, size = BACK[t]
        for k in range(size // GROUP):
            at = slice(first + k * GROUP, first + (k + 1) * GROUP)
            stacked = shares[:, at].reshape(N_RET * ENTRIES * GROUP, QUARTER)
            summed = dot(selector[...], stacked)
            owned[:, at] = summed.astype(BF16).reshape(N_HEAD * POOL_DEV, GROUP, QUARTER)
        first, size = BACK[t]
        here = pl.ds(first, size)
        for d in (1, 3, 2):
            own_copies.append(send(
                owned.at[pl.ds(over_head(d) * POOL_DEV, POOL_DEV), here], oenc.at[:, here, my_columns],
                s_own.at[t * 3 + d - 1], r_own.at[t * 3 + d - 1], (c, over_head(d), r),
            ))
        own_kept.append(keep(owned.at[pl.ds(h * POOL_DEV, POOL_DEV), here], oenc.at[:, here, my_columns]))

    back_copies, back_own = [], []
    share_copies = []
    flush(3 * CHUNKS)
    prepare_self()
    self_rows(0)
    self_rows(1)
    share_copies.append(share(0))
    self_rows(2)
    share_copies.append(share(1))
    self_rows(3)
    self_finish()
    share_copies.append(share(2))
    hand_back(0)
    back_copies, back_own = self_back()
    hand_back(1)
    hand_back(2)

    cross_done.wait()
    for copy in back_own + own_kept:
        copy.wait()
    for copy in back_copies + own_copies:
        copy.wait_recv()
    flush(0)


def place_outputs(own, cross, pool, *refs):
    targets, sem = refs[:5], refs[5]
    copies = [pltpu.make_async_copy(own.at[a], targets[a].at[0], sem.at[a]) for a in range(3)]
    copies.append(pltpu.make_async_copy(cross, targets[3], sem.at[3]))
    for b in range(POOL_DEV):
        copies.append(pltpu.make_async_copy(pool.at[b], targets[4].at[b], sem.at[4 + b]))
    for copy in copies:
        copy.start()
    for copy in copies:
        copy.wait()


def on_device(
    self_query, self_key, self_value, self_grad, self_docs, cross_query, cross_grad,
    neighbours, encodings, key_weight, value_weight,
):
    block = jax.ShapeDtypeStruct(self_query.shape, BF16)
    any_space = pl.BlockSpec(memory_space=pl.ANY)
    in_specs = [pl.BlockSpec(memory_space=pltpu.HBM)] * 11
    dma = pltpu.SemaphoreType.DMA
    wide = (ENTRIES, NR, key_weight.shape[1])
    scratch = [
        pltpu.SMEM(neighbours.shape, jnp.int32),
        pltpu.VMEM((N_RET, 8, 128), jnp.int32),
        pltpu.SMEM((N_RET, 8, 128), jnp.int32),
        pltpu.VMEM((1, BLOCK), jnp.int32),
        pltpu.VMEM((N_CTX * BLOCK, 128), F32),
        pltpu.VMEM((4 * BLOCK + DOC_ROWS, N_CTX * DH), BF16),
        tuple(pltpu.VMEM((N_HEAD * POOL_DEV, size, QUARTER), BF16) for _, size in FETCH),
        pltpu.VMEM((N_RET * ENTRIES, NR, QUARTER), BF16),
        tuple(pltpu.VMEM((N_RET * ENTRIES, size, QUARTER), BF16) for _, size in FETCH),
        pltpu.VMEM((ENTRIES, NR, E), BF16),
        pltpu.VMEM((N_CTX, 4 * BLOCK + DOC_ROWS, DH), BF16),
        pltpu.VMEM((N_CTX * BLOCK, DH), F32),
        pltpu.VMEM((N_CTX * BLOCK, DH), F32),
        pltpu.VMEM((3, N_CTX * BLOCK, DH), BF16),
        pltpu.VMEM(key_weight.shape, BF16),
        pltpu.VMEM(value_weight.shape, BF16),
        pltpu.VMEM(cross_query.shape[1:], BF16),
        pltpu.VMEM(cross_grad.shape[1:], BF16),
        pltpu.VMEM(cross_grad.shape[1:], BF16),
        pltpu.VMEM(wide, F32),
        pltpu.VMEM(wide, F32),
        pltpu.VMEM(wide, BF16),
        pltpu.VMEM(wide, BF16),
        pltpu.VMEM(wide, BF16),
        pltpu.VMEM(wide, BF16),
        pltpu.VMEM((N_HEAD, ENTRIES, NR, QUARTER), BF16),
        pltpu.VMEM((N_HEAD, ENTRIES, NR, QUARTER), BF16),
        pltpu.VMEM((N_RET * ENTRIES, NR, QUARTER), BF16),
        pltpu.VMEM((N_HEAD * POOL_DEV, NR, QUARTER), BF16),
        pltpu.VMEM((N_HEAD * POOL_DEV * 16, N_RET * ENTRIES * 16), BF16),
        dma((32,)),
        dma((3,)), dma((3,)),
        dma((3 * CHUNKS,)), dma((3 * CHUNKS,)),
        dma((3 * CHUNKS,)), dma((3 * CHUNKS,)),
        dma((3 * CHUNKS,)), dma((3 * CHUNKS,)),
        dma((7,)), dma((7,)),
        dma((3 * CHUNKS,)), dma((3 * CHUNKS,)),
        dma((3 * CHUNKS,)), dma((3 * CHUNKS,)),
        dma((3 * CHUNKS,)), dma((3 * CHUNKS,)),
        dma((7,)), dma((7,)),
    ]
    outs = pl.pallas_call(
        kernel,
        out_shape=(
            jax.ShapeDtypeStruct((3,) + self_query.shape[1:], BF16), block,
            jax.ShapeDtypeStruct(encodings.shape, BF16),
        ),
        in_specs=in_specs,
        out_specs=(any_space,) * 3,
        scratch_shapes=scratch,
        compiler_params=pltpu.CompilerParams(
            collective_id=0, has_side_effects=True, vmem_limit_bytes=32 * 2**20
        ),
        name="retro_backward",
    )(*[
        pltpu.with_memory_space_constraint(array, pltpu.HBM)
        for array in (self_query, self_key, self_value, self_grad, self_docs, cross_query, cross_grad)
    ], pltpu.with_memory_space_constraint(neighbours, pltpu.HBM), *[
        pltpu.with_memory_space_constraint(array, pltpu.HBM)
        for array in (encodings, key_weight, value_weight)
    ])
    return pl.pallas_call(
        place_outputs,
        out_shape=(block, block, block, block, jax.ShapeDtypeStruct(encodings.shape, BF16)),
        in_specs=[any_space] * 3,
        out_specs=(pl.BlockSpec(memory_space=pltpu.HBM),) * 5,
        scratch_shapes=[dma((4 + POOL_DEV,))],
        name="place_outputs",
    )(*[pltpu.with_memory_space_constraint(out, pltpu.VMEM) for out in outs])


def solution(mesh):
    tokens = P("ret", "ctx", "head")
    pool = P(("ctx", "head", "ret"), None, None)
    placed = (
        tokens, tokens, tokens, tokens, P("ret", "ctx"), tokens, tokens,
        P("ret", "ctx", None), pool, P(None, "head"), P(None, "head"),
    )
    return jax.shard_map(
        on_device,
        mesh=mesh,
        in_specs=placed,
        out_specs=(tokens, tokens, tokens, tokens, pool),
        check_vma=False,
    )
```
